128 devices in a mesh: dp: 1, seg: 16 (over y, x), head: 8 (over z, core).
Axes of the slice: x: 4, y: 4, z: 4, core: 2. Of those that a mesh axis runs over, the one named last changes fastest.
Arguments:
- inputs: bfloat16 [16384, 8192], P(('dp', 'seg', 'head')), may hold values from -6 to 6
- b_rows: bfloat16 [16384, 2048], P(('dp', 'seg', 'head')), may hold values from -0.375 to 0.375
- c_rows: bfloat16 [16384, 2048], P(('dp', 'seg', 'head')), may hold values from -0.375 to 0.375
- dt_rows: bfloat16 [16384, 128], P(('dp', 'seg', 'head')), may hold values from -1.5 to 1
- a_log: float32 [128], replicated, may hold values from -14 to -2, as said below
- d_skip: float32 [128], replicated, may hold values from 0.5 to 1.5
- grad_out: bfloat16 [16384, 8192], P(('dp', 'seg', 'head')), may hold values from -0.29882812 to 0.29882812
Outputs:
- outputs: bfloat16 [16384, 8192], P(('dp', 'seg', 'head'))
- grad_inputs: bfloat16 [16384, 8192], P(('dp', 'seg', 'head'))
- grad_b: bfloat16 [16384, 2048], P(('dp', 'seg', 'head'))
- grad_c: bfloat16 [16384, 2048], P(('dp', 'seg', 'head'))
- grad_dt: bfloat16 [16384, 128], P(('dp', 'seg', 'head'))
- grad_a_log: float32 [128], P(('dp', 'head'))
- grad_d_skip: float32 [128], P(('dp', 'head'))
The draws below stay inside these ranges and needn't reach their ends.
Inputs may be any that keep to these rules, and one draw needn't show every extreme that they name: a_log lies between log(0.1 / 16384) and log(1 / 12).
All inputs are finite; a program needn't handle non-finite values.
Results may differ from the reference program's by a relative error of at most 0.0014.
Values may be sent and summed in bfloat16 or wider, within the bound.
No kernel may reach another device: no remote copies, remote signals or barrier semaphores. Data moves between devices by JAX's collectives and lax.ppermute only.
A program may use at most 384 MiB of HBM per device.

```python
import jax
import jax.numpy as jnp
from jax import lax

HEADS = 128
HEAD_DIM = 64
GSTATE = 256
GROUPS = 8
BLOCK = 256
TOKENS = 16384


def draw_a_log(key, part):
    key = jax.random.fold_in(key, 7)
    pick_key, slow_key, fast_key = jax.random.split(key, 3)
    share = 0.5
    fast_heads = jax.random.uniform(pick_key, (HEADS,)) < share
    slower_decay_rate = jnp.log(0.1 / TOKENS) + jax.random.uniform(slow_key, (HEADS,)) * jnp.log(15.0)
    fast_rate = jnp.log(1.0 / 20.0) + jax.random.uniform(fast_key, (HEADS,)) * jnp.log(20.0 / 12.0)
    return jnp.where(fast_heads, fast_rate, slower_decay_rate).astype(jnp.float32)


def steps_of(stream_key, extent, cuts, low, top_value):
    def one(dim, shards_of):
        heights = jax.random.uniform(jax.random.fold_in(jax.random.fold_in(stream_key, 6), dim), (shards_of,), jnp.float32, low / len(cuts), top_value / len(cuts))
        return jnp.repeat(jnp.exp(heights), extent[dim] // shards_of).reshape((-1,) + (1,) * (len(extent) - dim - 1))

    level = one(*cuts[0])
    for cut in cuts[1:]:
        level = level * one(*cut)
    return level


def bell_draw(stream_key, extent, width, reach, cuts=(), held_as=jnp.bfloat16):
    factor_of = steps_of(stream_key, extent, cuts, -0.22, 0.18) if cuts else 1.0
    entries = jax.random.normal(stream_key, extent, jnp.float32) * width * factor_of
    return jnp.minimum(jnp.maximum(entries, -reach), reach).astype(held_as)


def setup_inputs(seed: int = 0, part: int = 0) -> dict:
    splits = jax.random.split(jax.random.key(seed), 8)
    part_splits = jax.random.split(jax.random.fold_in(splits[7], part), 8)
    return {
        "inputs": bell_draw(part_splits[0], (TOKENS, HEADS * HEAD_DIM), 1.0, 6.0, ((0, 128),)),
        "b_rows": bell_draw(part_splits[1], (TOKENS, GROUPS * GSTATE), GSTATE ** -0.5, 0.375, ((0, 128),)),
        "c_rows": bell_draw(part_splits[2], (TOKENS, GROUPS * GSTATE), GSTATE ** -0.5, 0.375, ((0, 128),)),
        "dt_rows": jnp.clip(-1.5 + 2.5 * jax.random.uniform(part_splits[3], (TOKENS, HEADS), jnp.float32) ** steps_of(part_splits[3], (TOKENS, HEADS), ((0, 128),), -0.2, 0.2), -1.5, 1.0).astype(jnp.bfloat16),
        "a_log": draw_a_log(jax.random.fold_in(splits[7], 71), part),
        "d_skip": jnp.clip(jax.random.uniform(splits[5], (HEADS,), jnp.float32, 0.5, 1.5), 0.5, 1.5),
        "grad_out": bell_draw(part_splits[6], (TOKENS, HEADS * HEAD_DIM), 0.05, 0.29882812, ((0, 128),)),
    }


HIGH_ACCURACY = lax.Precision.HIGHEST

def ssd_blocks(inputs, b_rows, c_rows, dt_rows, a_log, d_skip, state_init):
    head_count, head_width, state_width = state_init.shape
    groups = b_rows.shape[1] // state_width
    repeat = head_count // groups
    blocks = inputs.shape[0] // BLOCK
    x_blocks = inputs.reshape(blocks, BLOCK, groups, repeat, head_width)
    b_blocks = b_rows.reshape(blocks, BLOCK, groups, state_width)
    c_blocks = c_rows.reshape(blocks, BLOCK, groups, state_width)
    step_size_blocks = dt_rows.reshape(blocks, BLOCK, groups, repeat)
    decay_rate = jnp.exp(a_log).reshape(groups, repeat)
    skip_gain = d_skip.reshape(groups, repeat)
    causal = jnp.arange(BLOCK)[:, None] >= jnp.arange(BLOCK)[None, :]

    def advance(running, pieces):
        input_block, b_block, c_block, dt_block = pieces
        step_size = jax.nn.softplus(dt_block)
        cumulative = jnp.cumsum(-step_size * decay_rate, axis=0)
        along = jnp.moveaxis(cumulative, 0, -1)
        decay_gap = along[..., :, None] - along[..., None, :]
        mixing_weights = jnp.where(causal, jnp.exp(jnp.where(causal, decay_gap, 0.0)), 0.0)
        scores = jnp.einsum('tgn,sgn->gts', c_block, b_block, precision=HIGH_ACCURACY)
        mixing_weights = mixing_weights * scores[:, None] * jnp.moveaxis(step_size, 0, -1)[..., None, :]
        intra_block_part = jnp.einsum('mlbn,nmlc->bmlc', mixing_weights, input_block, precision=HIGH_ACCURACY)
        carried_over = jnp.einsum('tgn,grpn->tgrp', c_block, running, precision=HIGH_ACCURACY) * jnp.exp(cumulative)[..., None]
        tail_weight = jnp.exp(cumulative[-1][None] - cumulative) * step_size
        fresh_state = jnp.einsum('sgrp,sgn->grpn', input_block * tail_weight[..., None], b_block, precision=HIGH_ACCURACY)
        running = running * jnp.exp(cumulative[-1])[..., None, None] + fresh_state
        return (running, intra_block_part + carried_over + skip_gain[..., None] * input_block)
    running = state_init.reshape(groups, repeat, head_width, state_width)
    final_state, results = lax.scan(advance, running, (x_blocks, b_blocks, c_blocks, step_size_blocks))
    return (results.reshape(inputs.shape), final_state.reshape(head_count, head_width, state_width))

def reference(inputs, b_rows, c_rows, dt_rows, a_log, d_skip, grad_out):
    state_init = jnp.zeros((HEADS, HEAD_DIM, GSTATE), jnp.float32)

    def forward(x_float, b_float, c_float, dt_float, log_rate, skip_gain):
        return ssd_blocks(x_float, b_float, c_float, dt_float, log_rate, skip_gain, state_init)[0]
    results, pullback = jax.vjp(forward, inputs.astype(jnp.float32), b_rows.astype(jnp.float32), c_rows.astype(jnp.float32), dt_rows.astype(jnp.float32), a_log, d_skip)
    grads = pullback(grad_out.astype(jnp.float32))
    return (results.astype(jnp.bfloat16), grads[0].astype(jnp.bfloat16), grads[1].astype(jnp.bfloat16), grads[2].astype(jnp.bfloat16), grads[3].astype(jnp.bfloat16), grads[4], grads[5])
```

```python
import jax
import jax.numpy as jnp
from jax import lax
from jax.experimental import pallas as pl
from jax.experimental.pallas import tpu as pltpu
from jax.sharding import PartitionSpec as P

HEAD_DIM = 64
GSTATE = 256
BLOCK = 256
LANES = 128
VMEM_BYTES = 52 * 1024 * 1024

F32 = jnp.float32
BF16 = jnp.bfloat16


def dot(left, right):
    return lax.dot_general(left, right, (((1,), (0,)), ((), ())), preferred_element_type=F32)


def dot_nt(left, right):
    return lax.dot_general(left, right, (((1,), (1,)), ((), ())), preferred_element_type=F32)


def split2(value):
    high = value.astype(BF16)
    return high, (value - high.astype(F32)).astype(BF16)


def split3(value):
    high, rest = value.astype(BF16), None
    rest = value - high.astype(F32)
    middle = rest.astype(BF16)
    return high, middle, (rest - middle.astype(F32)).astype(BF16)


def dot3(ones, value):
    high, middle, low = split3(value)
    return dot(ones, high) + dot(ones, middle) + dot(ones, low)


def iota(shape, dim):
    return lax.broadcasted_iota(jnp.int32, shape, dim)


def step_sizes(dt_ref, rate_ref):
    dt = dt_ref[...].astype(F32)
    step = jnp.log(1.0 + jnp.exp(dt))
    log_decay = -step * rate_ref[...]
    lower = (iota((BLOCK, BLOCK), 0) >= iota((BLOCK, BLOCK), 1)).astype(BF16)
    return dt, step, log_decay, dot3(lower, log_decay)


def spread(value, heads, expand_ref):
    high, middle, low = split3(value)
    lane = iota(value.shape, 1)
    terms = jnp.where(lane < heads, high, jnp.where(lane < 2 * heads, middle, low))
    return dot(terms, expand_ref[...])


def gather_heads(value, collect_ref):
    high, low = split2(value)
    return dot(high, collect_ref[...]) + dot(low, collect_ref[...])


def state_kernel(heads, x_ref, b_ref, dt_ref, rate_ref, expand_ref, out_ref):
    @pl.when(pl.program_id(0) == 0)
    def _():
        out_ref[...] = jnp.zeros_like(out_ref)

    _, step, _, cumulative = step_sizes(dt_ref, rate_ref)
    weight = spread(jnp.exp(-cumulative) * step, heads, expand_ref)
    decay = spread(jnp.exp(cumulative[BLOCK - 8 :]), heads, expand_ref)[7:8]
    x_high, x_low = split2(x_ref[...].astype(F32) * weight)
    b_t = b_ref[...].T
    out_ref[...] = (out_ref[...] + dot(b_t, x_high) + dot(b_t, x_low)) * decay


def grad_state_kernel(heads, dy_ref, c_ref, dt_ref, rate_ref, expand_ref, out_ref):
    @pl.when(pl.program_id(0) == 0)
    def _():
        out_ref[...] = jnp.zeros_like(out_ref)

    _, _, _, cumulative = step_sizes(dt_ref, rate_ref)
    growth = spread(jnp.exp(cumulative), heads, expand_ref)
    dy_high, dy_low = split2(dy_ref[...].astype(F32) * growth)
    c_t = c_ref[...].T
    out_ref[...] = out_ref[...] * growth[BLOCK - 1 :] + dot(c_t, dy_high) + dot(c_t, dy_low)


def forward_kernel(
    heads, x_ref, b_ref, dt_ref, dy_ref, c_ref, start_ref, rate_ref, skip_ref, expand_ref, collect_ref,
    out_ref, states_ref, mixed_ref, dots_ref, skip_grad_ref, running,
):
    @pl.when(pl.program_id(0) == 0)
    def _():
        running[...] = start_ref[...]
        skip_grad_ref[...] = jnp.zeros_like(skip_grad_ref)

    channels = x_ref.shape[1]
    _, step, _, cumulative = step_sizes(dt_ref, rate_ref)
    growth = spread(jnp.exp(cumulative), heads, expand_ref)
    weight = spread(jnp.exp(-cumulative) * step, heads, expand_ref)
    x = x_ref[...].astype(F32)
    dy = dy_ref[...].astype(F32)
    b, c = b_ref[...], c_ref[...]
    state = running[...]
    states_ref[...] = state
    s_high, s_low = split2(state)
    x_high, x_low = split2(x * weight)
    causal = iota((BLOCK, BLOCK), 0) >= iota((BLOCK, BLOCK), 1)
    k_high, k_low = split2(jnp.where(causal, dot_nt(c, b), 0.0))
    inner = dot(k_high, x_high) + dot(k_high, x_low) + dot(k_low, x_high)
    inner = (inner + dot(c, s_high) + dot(c, s_low)) * growth
    out_ref[:, :channels] = (inner + skip_ref[...] * x).astype(BF16)
    dots_ref[...] = gather_heads(dy * inner, collect_ref)
    skip_grad_ref[...] += jnp.sum(dy * x, axis=0, keepdims=True)
    d_high, d_low = split2(dy * growth)
    mixed = dot_nt(d_high, x_high) + dot_nt(d_high, x_low) + dot_nt(d_low, x_high)
    mixed = jnp.where(causal, mixed, 0.0)
    mixed_ref[...] = mixed
    q_high, q_low = split2(mixed)
    grad_c = dot(q_high, b) + dot(q_low, b)
    grad_c = grad_c + dot_nt(d_high, s_high) + dot_nt(d_high, s_low) + dot_nt(d_low, s_high)
    out_ref[:, channels:] = grad_c.astype(BF16)
    b_t = b.T
    running[...] = (state + dot(b_t, x_high) + dot(b_t, x_low)) * growth[BLOCK - 1 :]


def backward_kernel(
    heads, x_ref, b_ref, dt_ref, dy_ref, c_ref, end_ref, states_ref, mixed_ref, dots_ref, rate_ref, skip_ref,
    expand_ref, collect_ref, out_ref, rate_grad_ref, running,
):
    @pl.when(pl.program_id(0) == 0)
    def _():
        running[...] = end_ref[...]
        rate_grad_ref[...] = jnp.zeros_like(rate_grad_ref)

    channels = x_ref.shape[1]
    width = b_ref.shape[1]
    dt, step, log_decay, cumulative = step_sizes(dt_ref, rate_ref)
    growth = spread(jnp.exp(cumulative), heads, expand_ref)
    weight = spread(jnp.exp(-cumulative) * step, heads, expand_ref)
    dy = dy_ref[...].astype(F32)
    b, c = b_ref[...], c_ref[...]
    scaled = x_ref[...].astype(F32) * weight
    x_high, x_low = split2(scaled)
    d_high, d_low = split2(dy * growth)
    later = running[...] * growth[BLOCK - 1 :]
    g_high, g_low = split2(later)
    causal = iota((BLOCK, BLOCK), 0) <= iota((BLOCK, BLOCK), 1)
    k_high, k_low = split2(jnp.where(causal, dot_nt(b, c), 0.0))
    inner = dot(k_high, d_high) + dot(k_high, d_low) + dot(k_low, d_high)
    inner = inner + dot(b, g_high) + dot(b, g_low)
    out_ref[:, :channels] = (inner * weight + skip_ref[...] * dy).astype(BF16)
    q_high, q_low = split2(mixed_ref[...].T)
    grad_b = dot(q_high, c) + dot(q_low, c)
    grad_b = grad_b + dot_nt(x_high, g_high) + dot_nt(x_high, g_low) + dot_nt(x_low, g_high)
    out_ref[:, channels : channels + width] = grad_b.astype(BF16)
    c_t = c.T
    earlier = later + dot(c_t, d_high) + dot(c_t, d_low)
    running[...] = earlier
    through = jnp.sum(earlier * states_ref[...], axis=0, keepdims=True)
    through = gather_heads(jnp.broadcast_to(through, (8, channels)), collect_ref)[:1]
    pulled = gather_heads(scaled * inner, collect_ref)
    below = (iota((BLOCK, BLOCK), 0) > iota((BLOCK, BLOCK), 1)).astype(BF16)
    grad_log_decay = through - dot3(below, dots_ref[...] - pulled)
    rate_grad_ref[...] += jnp.sum(grad_log_decay * log_decay, axis=0, keepdims=True)
    grad_step = pulled / step - rate_ref[...] * grad_log_decay
    out_ref[:, channels + width :] = (grad_step / (1.0 + jnp.exp(-dt))).astype(BF16)


def scan_kernel(backward, pieces_ref, decay_ref, out_ref):
    count = pieces_ref.shape[0]
    total = jnp.zeros(pieces_ref.shape[1:], F32)
    for index in reversed(range(count)) if backward else range(count):
        out_ref[index] = total
        total = total * decay_ref[index : index + 1] + pieces_ref[index]


def params():
    return pltpu.CompilerParams(vmem_limit_bytes=VMEM_BYTES, dimension_semantics=("arbitrary",))


def cost(flops, traffic):
    return pl.CostEstimate(flops=flops, bytes_accessed=traffic, transcendentals=0)


def seg_scan(state, decays, backward):
    count = lax.axis_size("seg")
    rows, channels = state.shape
    pieces = lax.all_to_all(state.reshape(count, rows // count, channels), "seg", 0, 0)
    sums = pl.pallas_call(
        lambda *refs: scan_kernel(backward, *refs),
        out_shape=jax.ShapeDtypeStruct(pieces.shape, F32),
        compiler_params=pltpu.CompilerParams(vmem_limit_bytes=VMEM_BYTES),
        cost_estimate=cost(2 * state.size, 8 * state.size),
    )(pieces, decays)
    return lax.all_to_all(sums, "seg", 0, 0).reshape(rows, channels)


def on_device(inputs, b_rows, c_rows, dt_rows, a_log, d_skip, grad_out):
    shards, segments = lax.axis_size("head"), lax.axis_size("seg")
    rows = inputs.shape[0]
    heads = dt_rows.shape[1] // shards
    channels = inputs.shape[1] // shards
    width = b_rows.shape[1] // shards
    copies = LANES // heads
    first = lax.axis_index("head") * heads
    rate = jnp.exp(a_log)
    rate_here = lax.dynamic_slice_in_dim(rate, first, heads, 0)
    skip_here = lax.dynamic_slice_in_dim(d_skip, first, heads, 0)

    def parts(value):
        return value.reshape(rows, shards, -1).transpose(1, 0, 2)

    def exchange(value):
        return lax.all_to_all(value, "head", 0, 0)

    dt_parts = jnp.tile(parts(dt_rows), (1, 1, copies))
    first_in = exchange(jnp.concatenate([parts(inputs), parts(b_rows), dt_parts], axis=2))
    second_in = exchange(jnp.concatenate([parts(grad_out), parts(c_rows)], axis=2))
    local_total = jnp.sum(-jax.nn.softplus(dt_rows.astype(F32)) * rate, axis=0)
    totals = lax.all_gather(local_total, ("seg", "head")).reshape(segments, shards, -1).sum(axis=1)
    decays = jnp.exp(lax.dynamic_slice_in_dim(totals, first, heads, 1))
    decays = jnp.repeat(decays, HEAD_DIM, axis=1)

    length = rows * shards
    blocks = length // BLOCK
    xbd = first_in.reshape(length, channels + width + LANES)
    dyc = second_in.reshape(length, channels + width)
    rate_row = jnp.tile(rate_here, copies)[None]
    skip_row = jnp.repeat(skip_here, HEAD_DIM)[None]
    lane, channel = jnp.arange(LANES), jnp.arange(channels)
    same = (lane % heads)[:, None] == (channel // HEAD_DIM)[None, :]
    expand = (same & (lane < 3 * heads)[:, None]).astype(BF16)
    collect = same.T.astype(BF16)

    def whole(array):
        return pl.BlockSpec(array.shape, lambda i: (0,) * array.ndim)

    def sections(place):
        return {
            "main": pl.BlockSpec((BLOCK, channels), lambda i: (place(i), 0)),
            "side": pl.BlockSpec((BLOCK, width), lambda i: (place(i), channels // width)),
            "dt": pl.BlockSpec((BLOCK, LANES), lambda i: (place(i), (channels + width) // LANES)),
            "per_head": pl.BlockSpec((BLOCK, LANES), lambda i: (place(i), 0)),
            "mixed": pl.BlockSpec((BLOCK, BLOCK), lambda i: (place(i), 0)),
            "state": pl.BlockSpec((None, width, channels), lambda i: (place(i), 0, 0)),
        }

    onward = sections(lambda i: i)
    back = sections(lambda i: blocks - 1 - i)
    state_shape = jax.ShapeDtypeStruct((width, channels), F32)
    unit = 2 * length * width * channels

    state = pl.pallas_call(
        lambda *refs: state_kernel(heads, *refs),
        grid=(blocks,),
        in_specs=[onward["main"], onward["side"], onward["dt"], whole(rate_row), whole(expand)],
        out_specs=pl.BlockSpec((width, channels), lambda i: (0, 0)),
        out_shape=state_shape,
        compiler_params=params(),
        cost_estimate=cost(2 * unit, 4 * length * channels),
    )(xbd, xbd, xbd, rate_row, expand)
    start = seg_scan(state, decays, False)
    grad_state = pl.pallas_call(
        lambda *refs: grad_state_kernel(heads, *refs),
        grid=(blocks,),
        in_specs=[back["main"], back["side"], back["dt"], whole(rate_row), whole(expand)],
        out_specs=pl.BlockSpec((width, channels), lambda i: (0, 0)),
        out_shape=state_shape,
        compiler_params=params(),
        cost_estimate=cost(2 * unit, 4 * length * channels),
    )(dyc, dyc, xbd, rate_row, expand)
    end = seg_scan(grad_state, decays, True)

    results, states, mixed, dots, skip_grad = pl.pallas_call(
        lambda *refs: forward_kernel(heads, *refs),
        grid=(blocks,),
        in_specs=[
            onward["main"], onward["side"], onward["dt"], onward["main"], onward["side"], whole(start),
            whole(rate_row), whole(skip_row), whole(expand), whole(collect),
        ],
        out_specs=[
            pl.BlockSpec((BLOCK, channels + width), lambda i: (i, 0)),
            onward["state"], onward["mixed"], onward["per_head"],
            pl.BlockSpec((1, channels), lambda i: (0, 0)),
        ],
        out_shape=[
            jax.ShapeDtypeStruct((length, channels + width), BF16),
            jax.ShapeDtypeStruct((blocks, width, channels), F32),
            jax.ShapeDtypeStruct((length, BLOCK), F32),
            jax.ShapeDtypeStruct((length, LANES), F32),
            jax.ShapeDtypeStruct((1, channels), F32),
        ],
        scratch_shapes=[pltpu.VMEM((width, channels), F32)],
        compiler_params=params(),
        cost_estimate=cost(14 * unit, 16 * length * channels),
    )(xbd, xbd, xbd, dyc, dyc, start, rate_row, skip_row, expand, collect)
    first_out = exchange(results.reshape(shards, rows, channels + width))

    grads, rate_grad = pl.pallas_call(
        lambda *refs: backward_kernel(heads, *refs),
        grid=(blocks,),
        in_specs=[
            back["main"], back["side"], back["dt"], back["main"], back["side"], whole(end),
            back["state"], back["mixed"], back["per_head"],
            whole(rate_row), whole(skip_row), whole(expand), whole(collect),
        ],
        out_specs=[
            pl.BlockSpec((BLOCK, channels + width + LANES), lambda i: (blocks - 1 - i, 0)),
            pl.BlockSpec((1, LANES), lambda i: (0, 0)),
        ],
        out_shape=[
            jax.ShapeDtypeStruct((length, channels + width + LANES), BF16),
            jax.ShapeDtypeStruct((1, LANES), F32),
        ],
        scratch_shapes=[pltpu.VMEM((width, channels), F32)],
        compiler_params=params(),
        cost_estimate=cost(12 * unit, 16 * length * channels),
    )(xbd, xbd, xbd, dyc, dyc, end, states, mixed, dots, rate_row, skip_row, expand, collect)
    second_out = exchange(grads.reshape(shards, rows, channels + width + LANES))

    skip_grad = skip_grad.reshape(heads, HEAD_DIM).sum(axis=1)
    sums = jnp.concatenate([rate_grad[0, :heads], skip_grad])
    sums = jnp.pad(sums, (0, LANES - 2 * heads))
    sums = lax.all_to_all(jnp.broadcast_to(sums, (segments, 1, LANES)), "seg", 0, 0).sum(axis=(0, 1))

    def whole_rows(value):
        return value.transpose(1, 0, 2).reshape(rows, -1)

    return (
        whole_rows(first_out[:, :, :channels]),
        whole_rows(second_out[:, :, :channels]),
        whole_rows(second_out[:, :, channels : channels + width]),
        whole_rows(first_out[:, :, channels:]),
        whole_rows(second_out[:, :, channels + width : channels + width + heads]),
        sums[:heads],
        sums[heads : 2 * heads],
    )


def solution(mesh):
    by_rows = P(("dp", "seg", "head"), None)
    in_specs = (by_rows, by_rows, by_rows, by_rows, P(), P(), by_rows)
    out_specs = (by_rows, by_rows, by_rows, by_rows, by_rows, P(("dp", "head")), P(("dp", "head")))
    return jax.shard_map(on_device, mesh=mesh, in_specs=in_specs, out_specs=out_specs, check_vma=False)
```

```python
import jax
import jax.numpy as jnp
from jax import lax
from jax.experimental import pallas as pl
from jax.experimental.pallas import tpu as pltpu
from jax.sharding import PartitionSpec as P

HEAD_DIM = 64
GSTATE = 256
BLOCK = 256
LANES = 128
CHUNK = 256
VMEM_BYTES = 52 * 1024 * 1024

F32 = jnp.float32
BF16 = jnp.bfloat16


def dot(left, right):
    return lax.dot_general(left, right, (((1,), (0,)), ((), ())), preferred_element_type=F32)


def dot_nt(left, right):
    return lax.dot_general(left, right, (((1,), (1,)), ((), ())), preferred_element_type=F32)


def split2(value):
    high = value.astype(BF16)
    return high, (value - high.astype(F32)).astype(BF16)


def split3(value):
    high, rest = value.astype(BF16), None
    rest = value - high.astype(F32)
    middle = rest.astype(BF16)
    return high, middle, (rest - middle.astype(F32)).astype(BF16)


def dot3(ones, value):
    high, middle, low = split3(value)
    return dot(ones, high) + dot(ones, middle) + dot(ones, low)


def iota(shape, dim):
    return lax.broadcasted_iota(jnp.int32, shape, dim)


def step_sizes(dt, rate):
    step = jnp.log(1.0 + jnp.exp(dt))
    return step, -step * rate


def three_terms(value, heads):
    high, middle, low = split3(value)
    lane = iota(value.shape, 1)
    return jnp.where(lane < heads, high, jnp.where(lane < 2 * heads, middle, low))


def chunks(channels):
    return [slice(at, at + CHUNK) for at in range(0, channels, CHUNK)]


def gather_heads(value, collect):
    high, low = split2(value)
    return dot(high, collect) + dot(low, collect)


def pack_kernel(heads, x_ref, b_ref, dt_ref, out_ref):
    shard, channels, width = pl.program_id(0), x_ref.shape[1], b_ref.shape[1]
    out_ref[:, :channels] = x_ref[...]
    out_ref[:, channels : channels + width] = b_ref[...]
    wanted = shard * heads + lax.rem(iota((LANES, LANES), 1), heads)
    pick = (iota((LANES, LANES), 0) == wanted).astype(BF16)
    out_ref[:, channels + width :] = dot(dt_ref[...], pick).astype(BF16)


def unpack_kernel(heads, in_ref, x_ref, b_ref, dt_ref):
    shard, channels, width = pl.program_id(0), x_ref.shape[1], b_ref.shape[1]
    x_ref[...] = in_ref[:, :channels]
    b_ref[...] = in_ref[:, channels : channels + width]
    mine = iota(dt_ref.shape, 1) // heads == shard
    dt_ref[...] = jnp.where(mine, in_ref[:, channels + width :], dt_ref[...])


def state_kernel(heads, x_ref, b_ref, dt_ref, rate_ref, expand_ref, out_ref, growth_ref, weight_ref):
    block = pl.program_id(0)
    channels = x_ref.shape[1]

    @pl.when(block == 0)
    def _():
        out_ref[...] = jnp.zeros_like(out_ref)
        lower = (iota((BLOCK, BLOCK), 0) >= iota((BLOCK, BLOCK), 1)).astype(BF16)
        log_total = jnp.zeros((1, LANES), F32)
        for at in range(0, dt_ref.shape[0], BLOCK):
            rows = slice(at, at + BLOCK)
            step, log_decay = step_sizes(dt_ref[rows].astype(F32), rate_ref[...])
            cumulative = dot3(lower, log_decay)
            growth_ref[rows] = three_terms(jnp.exp(cumulative), heads)
            weight_ref[rows] = three_terms(jnp.exp(-cumulative) * step, heads)
            log_total = log_total + cumulative[BLOCK - 1 :]
        out_ref[:, channels:] = jnp.broadcast_to(jnp.exp(log_total), (out_ref.shape[0], LANES))

    rows = pl.ds(pl.multiple_of(block * BLOCK, BLOCK), BLOCK)
    ends = pl.ds(pl.multiple_of(block * BLOCK + BLOCK - 16, 16), 16)
    weight, last = weight_ref[rows, :], growth_ref[ends, :]
    b_t = b_ref[...].T
    for part in chunks(channels):
        spread = expand_ref[:, part]
        high, low = split2(x_ref[:, part].astype(F32) * dot(weight, spread))
        decay = dot(last, spread)[15:]
        out_ref[:, part] = (out_ref[:, part] + dot(b_t, high) + dot(b_t, low)) * decay


def grad_state_kernel(pieces, growth_ref, expand_ref, *refs):
    piece_refs, (out_ref, dyc_ref) = refs[:pieces], refs[pieces:]
    channels = out_ref.shape[1]
    me = lax.axis_index("head")
    block = pl.num_programs(0) - 1 - pl.program_id(0)
    hop = lax.rem(me // 2 - block + pieces, pieces)

    @pl.when(pl.program_id(0) == 0)
    def _():
        out_ref[...] = jnp.zeros_like(out_ref)

    for index, piece_ref in enumerate(piece_refs):
        @pl.when(hop == index)
        def _():
            dyc_ref[...] = piece_ref[...]

    growth = growth_ref[...]
    c_t = dyc_ref[:, channels:].T
    for part in chunks(channels):
        grow = dot(growth, expand_ref[:, part])
        high, low = split2(dyc_ref[:, part].astype(F32) * grow)
        out_ref[:, part] = out_ref[:, part] * grow[BLOCK - 1 :] + dot(c_t, high) + dot(c_t, low)


def forward_kernel(
    x_ref, b_ref, dy_ref, c_ref, growth_ref, weight_ref, start_ref, skip_ref, expand_ref, collect_ref,
    out_ref, states_ref, mixed_ref, dots_ref, skip_grad_ref, running,
):
    @pl.when(pl.program_id(0) == 0)
    def _():
        running[...] = start_ref[...]
        skip_grad_ref[...] = jnp.zeros_like(skip_grad_ref)

    channels = x_ref.shape[1]
    b, c, growth, weight = b_ref[...], c_ref[...], growth_ref[...], weight_ref[...]
    b_t = b.T
    causal = iota((BLOCK, BLOCK), 0) >= iota((BLOCK, BLOCK), 1)
    k_high, k_low = split2(jnp.where(causal, dot_nt(c, b), 0.0))
    mixed = jnp.zeros((BLOCK, BLOCK), F32)
    grad_c = jnp.zeros(b.shape, F32)
    dots = jnp.zeros((BLOCK, LANES), F32)
    for part in chunks(channels):
        spread = expand_ref[:, part]
        grow = dot(growth, spread)
        x = x_ref[:, part].astype(F32)
        dy = dy_ref[:, part].astype(F32)
        x_high, x_low = split2(x * dot(weight, spread))
        d_high, d_low = split2(dy * grow)
        state = running[:, part]
        states_ref[:, part] = state
        s_high, s_low = split2(state)
        inner = dot(k_high, x_high) + dot(k_high, x_low) + dot(k_low, x_high) + dot(c, s_high) + dot(c, s_low)
        inner = inner * grow
        out_ref[:, part] = (inner + skip_ref[:, part] * x).astype(BF16)
        dots += gather_heads(dy * inner, collect_ref[part])
        skip_grad_ref[:, part] += jnp.sum(dy * x, axis=0, keepdims=True)
        mixed += dot_nt(d_high, x_high) + dot_nt(d_high, x_low) + dot_nt(d_low, x_high)
        grad_c += dot_nt(d_high, s_high) + dot_nt(d_high, s_low) + dot_nt(d_low, s_high)
        running[:, part] = (state + dot(b_t, x_high) + dot(b_t, x_low)) * grow[BLOCK - 1 :]
    dots_ref[...] = dots
    mixed = jnp.where(causal, mixed, 0.0)
    mixed_ref[...] = mixed
    q_high, q_low = split2(mixed)
    out_ref[:, channels:] = (grad_c + dot(q_high, b) + dot(q_low, b)).astype(BF16)


def backward_kernel(
    x_ref, b_ref, dt_ref, dy_ref, c_ref, growth_ref, weight_ref, end_ref, states_ref, mixed_ref, dots_ref, rate_ref,
    skip_ref, expand_ref, collect_ref, out_ref, rate_grad_ref, running,
):
    @pl.when(pl.program_id(0) == 0)
    def _():
        running[...] = end_ref[...]
        rate_grad_ref[...] = jnp.zeros_like(rate_grad_ref)

    channels, width = x_ref.shape[1], b_ref.shape[1]
    b, c, growth, weight = b_ref[...], c_ref[...], growth_ref[...], weight_ref[...]
    c_t = c.T
    anticausal = iota((BLOCK, BLOCK), 0) <= iota((BLOCK, BLOCK), 1)
    k_high, k_low = split2(jnp.where(anticausal, dot_nt(b, c), 0.0))
    q_high, q_low = split2(mixed_ref[...].T)
    grad_b = dot(q_high, c) + dot(q_low, c)
    pulled = jnp.zeros((BLOCK, LANES), F32)
    through = jnp.zeros((8, LANES), F32)
    for part in chunks(channels):
        spread, collect = expand_ref[:, part], collect_ref[part]
        grow, weigh = dot(growth, spread), dot(weight, spread)
        dy = dy_ref[:, part].astype(F32)
        scaled = x_ref[:, part].astype(F32) * weigh
        x_high, x_low = split2(scaled)
        d_high, d_low = split2(dy * grow)
        later = running[:, part] * grow[BLOCK - 1 :]
        g_high, g_low = split2(later)
        inner = dot(k_high, d_high) + dot(k_high, d_low) + dot(k_low, d_high) + dot(b, g_high) + dot(b, g_low)
        out_ref[:, part] = (inner * weigh + skip_ref[:, part] * dy).astype(BF16)
        grad_b += dot_nt(x_high, g_high) + dot_nt(x_high, g_low) + dot_nt(x_low, g_high)
        earlier = later + dot(c_t, d_high) + dot(c_t, d_low)
        running[:, part] = earlier
        meet = jnp.sum(earlier * states_ref[:, part], axis=0, keepdims=True)
        through += gather_heads(jnp.broadcast_to(meet, (8, CHUNK)), collect)
        pulled += gather_heads(scaled * inner, collect)
    out_ref[:, channels : channels + width] = grad_b.astype(BF16)
    dt = dt_ref[...].astype(F32)
    step, log_decay = step_sizes(dt, rate_ref[...])
    below = (iota((BLOCK, BLOCK), 0) > iota((BLOCK, BLOCK), 1)).astype(BF16)
    grad_log_decay = through[:1] - dot3(below, dots_ref[...] - pulled)
    rate_grad_ref[...] += jnp.sum(grad_log_decay * log_decay, axis=0, keepdims=True)
    grad_step = pulled / step - rate_ref[...] * grad_log_decay
    out_ref[:, channels + width :] = (grad_step / (1.0 + jnp.exp(-dt))).astype(BF16)


def scan_kernel(heads, pieces_ref, expand_ref, out_ref, decay_ref):
    count, channels = out_ref.shape[0], out_ref.shape[2]
    decay_ref[...] = dot(three_terms(pieces_ref[:, 0, channels:], heads), expand_ref[...])
    total = jnp.zeros(out_ref.shape[1:], F32)
    for index in range(count):
        out_ref[index] = total
        total = total * decay_ref[index : index + 1] + pieces_ref[index, :, :channels]


def back_scan_kernel(pieces_ref, decay_ref, out_ref):
    total = jnp.zeros(out_ref.shape[1:], F32)
    for index in reversed(range(out_ref.shape[0])):
        out_ref[index] = total
        total = total * decay_ref[index : index + 1] + pieces_ref[index]


def params():
    return pltpu.CompilerParams(vmem_limit_bytes=VMEM_BYTES, dimension_semantics=("arbitrary",))


def cost(flops, traffic):
    return pl.CostEstimate(flops=flops, bytes_accessed=traffic, transcendentals=0)


def seg_exchange(state):
    count = lax.axis_size("seg")
    return lax.all_to_all(state.reshape(count, -1, state.shape[-1]), "seg", 0, 0)


def seg_sum(value):
    count, hop = lax.axis_size("seg"), 1
    while hop < count:
        value = value + lax.ppermute(value, "seg", [(i, i ^ hop) for i in range(count)])
        hop *= 2
    return value


def exchange(value):
    return lax.all_to_all(value, "head", 0, 0)


def swap_cores(own, other):
    count, core = lax.axis_size("head"), lax.axis_index("head") % 2
    swapped = lax.ppermute(other, "head", [(i, i ^ 1) for i in range(count)])
    return jnp.stack([jnp.where(core == 0, own, swapped), jnp.where(core == 0, swapped, own)], axis=1)


def by_core(value):
    pairs, core = value.reshape(-1, 2, *value.shape[1:]), lax.axis_index("head") % 2
    pick = lambda place: lax.dynamic_index_in_dim(pairs, place, 1, keepdims=False)
    return pick(core), pick(1 - core)


def swap_chips(pairs, after):
    count, chip = lax.axis_size("head"), lax.axis_index("head") // 2
    chips = count // 2
    sent = [lax.dynamic_index_in_dim(pairs, (chip + hop) % chips, 0, keepdims=False) for hop in range(chips)]
    sent = [part.reshape(-1, part.shape[-1]) for part in sent]
    if after is not None:
        sent, _ = lax.optimization_barrier((sent, after))
    return sent[:1] + [
        lax.ppermute(sent[hop], "head", [(i, (i + 2 * hop) % count) for i in range(count)]) for hop in range(1, chips)
    ]


def on_device(inputs, b_rows, c_rows, dt_rows, a_log, d_skip, grad_out):
    shards, segments = lax.axis_size("head"), lax.axis_size("seg")
    rows = inputs.shape[0]
    heads = dt_rows.shape[1] // shards
    channels = inputs.shape[1] // shards
    width = b_rows.shape[1] // shards
    copies = LANES // heads
    first = lax.axis_index("head") * heads
    rate = jnp.exp(a_log)
    rate_here = lax.dynamic_slice_in_dim(rate, first, heads, 0)
    skip_here = lax.dynamic_slice_in_dim(d_skip, first, heads, 0)

    def parts(value):
        return value.reshape(rows, shards, -1).transpose(1, 0, 2)

    packed_width = channels + width + LANES
    packed = pl.pallas_call(
        lambda *refs: pack_kernel(heads, *refs),
        grid=(shards,),
        in_specs=[
            pl.BlockSpec((rows, channels), lambda i: (0, i)),
            pl.BlockSpec((rows, width), lambda i: (0, i)),
            pl.BlockSpec((rows, LANES), lambda i: (0, 0)),
        ],
        out_specs=pl.BlockSpec((None, rows, packed_width), lambda i: (i, 0, 0)),
        out_shape=jax.ShapeDtypeStruct((shards, rows, packed_width), BF16),
        compiler_params=params(),
        cost_estimate=cost(rows, 4 * shards * rows * packed_width),
    )(inputs, b_rows, dt_rows)
    first_in = exchange(packed)
    second_parts = jnp.concatenate([parts(grad_out), parts(c_rows)], axis=2)
    second_in = swap_chips(swap_cores(*by_core(second_parts)), first_in)

    length = rows * shards
    blocks = length // BLOCK
    xbd = first_in.reshape(length, packed_width)
    rate_row = jnp.tile(rate_here, copies)[None]
    skip_row = jnp.repeat(skip_here, HEAD_DIM)[None]
    lane, channel = jnp.arange(LANES), jnp.arange(channels)
    same = (lane % heads)[:, None] == (channel // HEAD_DIM)[None, :]
    expand = (same & (lane < 3 * heads)[:, None]).astype(BF16)
    collect = same.T.astype(BF16)

    def whole(array):
        return pl.BlockSpec(array.shape, lambda i: (0,) * array.ndim)

    def sections(place):
        return {
            "main": pl.BlockSpec((BLOCK, channels), lambda i: (place(i), 0)),
            "side": pl.BlockSpec((BLOCK, width), lambda i: (place(i), channels // width)),
            "dt": pl.BlockSpec((BLOCK, LANES), lambda i: (place(i), (channels + width) // LANES)),
            "per_head": pl.BlockSpec((BLOCK, LANES), lambda i: (place(i), 0)),
            "mixed": pl.BlockSpec((BLOCK, BLOCK), lambda i: (place(i), 0)),
            "state": pl.BlockSpec((None, width, channels), lambda i: (place(i), 0, 0)),
        }

    onward = sections(lambda i: i)
    back = sections(lambda i: blocks - 1 - i)
    state_shape = jax.ShapeDtypeStruct((width, channels), F32)
    unit = 2 * length * width * channels

    terms_shape = jax.ShapeDtypeStruct((length, LANES), BF16)
    state, growth, weight = pl.pallas_call(
        lambda *refs: state_kernel(heads, *refs),
        grid=(blocks,),
        in_specs=[
            onward["main"], onward["side"],
            pl.BlockSpec((length, LANES), lambda i: (0, (channels + width) // LANES)),
            whole(rate_row), whole(expand),
        ],
        out_specs=[
            pl.BlockSpec((width, channels + LANES), lambda i: (0, 0)),
            pl.BlockSpec((length, LANES), lambda i: (0, 0)),
            pl.BlockSpec((length, LANES), lambda i: (0, 0)),
        ],
        out_shape=[jax.ShapeDtypeStruct((width, channels + LANES), F32), terms_shape, terms_shape],
        compiler_params=params(),
        cost_estimate=cost(8 * unit, 4 * length * channels),
    )(xbd, xbd, xbd, rate_row, expand)
    piece = (segments, width // segments, channels)
    starts, decays = pl.pallas_call(
        lambda *refs: scan_kernel(heads, *refs),
        out_shape=[jax.ShapeDtypeStruct(piece, F32), jax.ShapeDtypeStruct((segments, channels), F32)],
        compiler_params=pltpu.CompilerParams(vmem_limit_bytes=VMEM_BYTES),
        cost_estimate=cost(unit, 8 * width * channels),
    )(seg_exchange(state), expand)
    start = seg_exchange(starts).reshape(width, channels)
    second_in, _ = lax.optimization_barrier((second_in, starts))
    piece_spec = pl.BlockSpec((BLOCK, channels + width), lambda i: (0, 0))
    grad_state, dyc = pl.pallas_call(
        lambda *refs: grad_state_kernel(len(second_in), *refs),
        grid=(blocks,),
        in_specs=[back["per_head"], whole(expand)] + [piece_spec] * len(second_in),
        out_specs=[
            pl.BlockSpec((width, channels), lambda i: (0, 0)),
            pl.BlockSpec((BLOCK, channels + width), lambda i: (blocks - 1 - i, 0)),
        ],
        out_shape=[state_shape, jax.ShapeDtypeStruct((length, channels + width), BF16)],
        compiler_params=params(),
        cost_estimate=cost(8 * unit, 4 * length * channels),
    )(growth, expand, *second_in)
    grad_state, _ = lax.optimization_barrier((grad_state, start))
    ends = pl.pallas_call(
        back_scan_kernel,
        out_shape=jax.ShapeDtypeStruct(piece, F32),
        compiler_params=pltpu.CompilerParams(vmem_limit_bytes=VMEM_BYTES),
        cost_estimate=cost(unit, 8 * width * channels),
    )(seg_exchange(grad_state), decays)
    end = seg_exchange(ends).reshape(width, channels)

    results, states, mixed, dots, skip_grad = pl.pallas_call(
        forward_kernel,
        grid=(blocks,),
        in_specs=[
            onward["main"], onward["side"], onward["main"], onward["side"], onward["per_head"], onward["per_head"],
            whole(start), whole(skip_row), whole(expand), whole(collect),
        ],
        out_specs=[
            pl.BlockSpec((BLOCK, channels + width), lambda i: (i, 0)),
            onward["state"], onward["mixed"], onward["per_head"],
            pl.BlockSpec((1, channels), lambda i: (0, 0)),
        ],
        out_shape=[
            jax.ShapeDtypeStruct((length, channels + width), BF16),
            jax.ShapeDtypeStruct((blocks, width, channels), F32),
            jax.ShapeDtypeStruct((length, BLOCK), F32),
            jax.ShapeDtypeStruct((length, LANES), F32),
            jax.ShapeDtypeStruct((1, channels), F32),
        ],
        scratch_shapes=[pltpu.VMEM((width, channels), F32)],
        compiler_params=params(),
        cost_estimate=cost(40 * unit, 16 * length * channels),
    )(xbd, xbd, dyc, dyc, growth, weight, start, skip_row, expand, collect)
    results, _ = lax.optimization_barrier((results, ends))
    first_out = swap_chips(swap_cores(*by_core(results.reshape(shards, rows, channels + width))), None)

    grads, rate_grad = pl.pallas_call(
        backward_kernel,
        grid=(blocks,),
        in_specs=[
            back["main"], back["side"], back["dt"], back["main"], back["side"], back["per_head"], back["per_head"],
            whole(end), back["state"], back["mixed"], back["per_head"],
            whole(rate_row), whole(skip_row), whole(expand), whole(collect),
        ],
        out_specs=[
            pl.BlockSpec((BLOCK, channels + width + LANES), lambda i: (blocks - 1 - i, 0)),
            pl.BlockSpec((1, LANES), lambda i: (0, 0)),
        ],
        out_shape=[
            jax.ShapeDtypeStruct((length, channels + width + LANES), BF16),
            jax.ShapeDtypeStruct((1, LANES), F32),
        ],
        scratch_shapes=[pltpu.VMEM((width, channels), F32)],
        compiler_params=params(),
        cost_estimate=cost(34 * unit, 16 * length * channels),
    )(xbd, xbd, xbd, dyc, dyc, growth, weight, end, states, mixed, dots, rate_row, skip_row, expand, collect)
    grads, _ = lax.optimization_barrier((grads, first_out[1:]))
    second_out = exchange(grads.reshape(shards, rows, channels + width + LANES))

    skip_grad = skip_grad.reshape(heads, HEAD_DIM).sum(axis=1)
    sums = jnp.concatenate([rate_grad[0, :heads], skip_grad])
    sums = seg_sum(jnp.pad(sums, (0, LANES - 2 * heads))[None])[0]

    grad_x, grad_b, grad_dt = pl.pallas_call(
        lambda *refs: unpack_kernel(heads, *refs),
        grid=(shards,),
        in_specs=[pl.BlockSpec((None, rows, packed_width), lambda i: (i, 0, 0))],
        out_specs=[
            pl.BlockSpec((rows, channels), lambda i: (0, i)),
            pl.BlockSpec((rows, width), lambda i: (0, i)),
            pl.BlockSpec((rows, LANES), lambda i: (0, 0)),
        ],
        out_shape=[jax.ShapeDtypeStruct(like.shape, BF16) for like in (inputs, b_rows, dt_rows)],
        compiler_params=params(),
        cost_estimate=cost(rows, 4 * shards * rows * packed_width),
    )(second_out)

    chip = lax.axis_index("head") // 2
    outputs = jnp.stack(first_out).reshape(len(first_out), 2, rows, channels + width)
    outputs = outputs[(chip - jnp.arange(len(first_out))) % len(first_out)]
    outputs = outputs.transpose(2, 0, 1, 3)
    return (
        outputs[..., :channels].reshape(rows, -1),
        grad_x,
        grad_b,
        outputs[..., channels:].reshape(rows, -1),
        grad_dt,
        sums[:heads],
        sums[heads : 2 * heads],
    )


def solution(mesh):
    by_rows = P(("dp", "seg", "head"), None)
    in_specs = (by_rows, by_rows, by_rows, by_rows, P(), P(), by_rows)
    out_specs = (by_rows, by_rows, by_rows, by_rows, by_rows, P(("dp", "head")), P(("dp", "head")))
    return jax.shard_map(on_device, mesh=mesh, in_specs=in_specs, out_specs=out_specs, check_vma=False)
```

```python
import jax
import jax.numpy as jnp
from jax import lax
from jax.experimental import pallas as pl
from jax.experimental.pallas import tpu as pltpu
from jax.sharding import PartitionSpec as P

HEAD_DIM = 64
GSTATE = 256
BLOCK = 256
LANES = 128
CHANNELS = 1024
VMEM_BYTES = 50 * 1024 * 1024

F32 = jnp.float32
BF16 = jnp.bfloat16


def dot(left, right):
    return lax.dot_general(left, right, (((1,), (0,)), ((), ())), preferred_element_type=F32)


def dot_nt(left, right):
    return lax.dot_general(left, right, (((1,), (1,)), ((), ())), preferred_element_type=F32)


def split2(value):
    high = value.astype(BF16)
    return high, (value - high.astype(F32)).astype(BF16)


def split3(value):
    high, rest = value.astype(BF16), None
    rest = value - high.astype(F32)
    middle = rest.astype(BF16)
    return high, middle, (rest - middle.astype(F32)).astype(BF16)


def dot3(ones, value):
    high, middle, low = split3(value)
    return dot(ones, high) + dot(ones, middle) + dot(ones, low)


def iota(shape, dim):
    return lax.broadcasted_iota(jnp.int32, shape, dim)


def step_sizes(dt, rate):
    step = jnp.log(1.0 + jnp.exp(dt))
    return step, -step * rate


def three_terms(value, heads):
    high, middle, low = split3(value)
    lane = iota(value.shape, 1)
    return jnp.where(lane < heads, high, jnp.where(lane < 2 * heads, middle, low))


def gather_heads(value, collect):
    high, low = split2(value)
    return dot(high, collect) + dot(low, collect)


def pack_kernel(heads, x_ref, b_ref, dt_ref, out_ref):
    here, channels, width = out_ref.shape[0], CHANNELS, GSTATE
    for index in range(here):
        shard = pl.program_id(0) * here + index
        out_ref[index, :, :channels] = x_ref[:, index * channels : (index + 1) * channels]
        out_ref[index, :, channels : channels + width] = b_ref[:, index * width : (index + 1) * width]
        wanted = shard * heads + lax.rem(iota((LANES, LANES), 1), heads)
        pick = (iota((LANES, LANES), 0) == wanted).astype(BF16)
        out_ref[index, :, channels + width :] = dot(dt_ref[...], pick).astype(BF16)


def unpack_kernel(heads, in_ref, x_ref, b_ref, dt_ref):
    here, channels, width = in_ref.shape[0], CHANNELS, GSTATE
    for index in range(here):
        shard = pl.program_id(0) * here + index
        x_ref[:, index * channels : (index + 1) * channels] = in_ref[index, :, :channels]
        b_ref[:, index * width : (index + 1) * width] = in_ref[index, :, channels : channels + width]
        mine = iota(dt_ref.shape, 1) // heads == shard
        dt_ref[...] = jnp.where(mine, in_ref[index, :, channels + width :], dt_ref[...])


def core_halves(first, second, own_ref, other_ref):
    core = lax.rem(lax.axis_index("head"), 2)

    @pl.when(core == 0)
    def _():
        own_ref[...], other_ref[...] = first, second

    @pl.when(core == 1)
    def _():
        own_ref[...], other_ref[...] = second, first


def pack_pair_kernel(dy_ref, c_ref, own_ref, other_ref):
    channels, width = CHANNELS, GSTATE
    first = jnp.concatenate([dy_ref[:, :channels], c_ref[:, :width]], axis=1)
    second = jnp.concatenate([dy_ref[:, channels:], c_ref[:, width:]], axis=1)
    core_halves(first, second, own_ref, other_ref)


def merge_kernel(own_ref, swapped_ref, *out_refs):
    me, chips, rows = lax.axis_index("head"), own_ref.shape[0], own_ref.shape[1]
    core = lax.rem(me, 2)
    for hop, out_ref in enumerate(out_refs):
        chip = lax.rem(me // 2 + hop, chips)
        out_ref[pl.ds(pl.multiple_of(core * rows, rows), rows), :] = own_ref[chip]
        out_ref[pl.ds(pl.multiple_of((1 - core) * rows, rows), rows), :] = swapped_ref[chip]


def unpack_pairs_kernel(pieces, *refs):
    piece_refs, (y_ref, c_ref) = refs[:pieces], refs[pieces:]
    me, rows, channels, width = lax.axis_index("head"), y_ref.shape[0], CHANNELS, GSTATE
    for hop, piece_ref in enumerate(piece_refs):
        chip = lax.rem(me // 2 - hop + pieces, pieces)
        for core in range(2):
            part = slice(core * rows, (core + 1) * rows)
            at = pl.multiple_of((2 * chip + core) * channels, channels)
            y_ref[:, pl.ds(at, channels)] = piece_ref[part, :channels]
            at = pl.multiple_of((2 * chip + core) * width, width)
            c_ref[:, pl.ds(at, width)] = piece_ref[part, channels:]


def state_kernel(
    heads, x_ref, b_ref, dt_ref, rate_ref, expand_ref,
    out_ref, growth_ref, weight_ref, before_ref, decay_ref, so_far,
):
    block = pl.program_id(0)
    channels = x_ref.shape[1]

    @pl.when(block == 0)
    def _():
        out_ref[...] = jnp.zeros_like(out_ref)
        so_far[...] = jnp.ones_like(so_far)
        lower = (iota((BLOCK, BLOCK), 0) >= iota((BLOCK, BLOCK), 1)).astype(BF16)
        log_total = jnp.zeros((1, LANES), F32)
        for at in range(0, dt_ref.shape[0], BLOCK):
            rows = slice(at, at + BLOCK)
            step, log_decay = step_sizes(dt_ref[rows].astype(F32), rate_ref[...])
            cumulative = dot3(lower, log_decay)
            growth_ref[rows] = three_terms(jnp.exp(cumulative), heads)
            weight_ref[rows] = three_terms(jnp.exp(-cumulative) * step, heads)
            log_total = log_total + cumulative[BLOCK - 1 :]
        out_ref[:, channels:] = jnp.broadcast_to(jnp.exp(log_total), (out_ref.shape[0], LANES))

    rows = pl.ds(pl.multiple_of(block * BLOCK, BLOCK), BLOCK)
    ends = pl.ds(pl.multiple_of(block * BLOCK + BLOCK - 16, 16), 16)
    spread = expand_ref[...]
    high, low = split2(x_ref[...].astype(F32) * dot(weight_ref[rows, :], spread))
    decay = dot(growth_ref[ends, :], spread)[15:]
    b_t = b_ref[...].T
    state = out_ref[:, :channels]
    before_ref[...] = state
    decay_ref[...] = so_far[...]
    so_far[...] = so_far[...] * decay
    out_ref[:, :channels] = (state + dot(b_t, high) + dot(b_t, low)) * decay


def grad_state_kernel(pieces, growth_ref, expand_ref, *refs):
    piece_refs, (out_ref, dyc_ref, later_ref, decay_ref, so_far) = refs[:pieces], refs[pieces:]
    channels = out_ref.shape[1]
    block = pl.num_programs(0) - 1 - pl.program_id(0)
    hop = lax.rem(lax.axis_index("head") // 2 - block + pieces, pieces)

    @pl.when(pl.program_id(0) == 0)
    def _():
        out_ref[...] = jnp.zeros_like(out_ref)
        so_far[...] = jnp.ones_like(so_far)

    for index, piece_ref in enumerate(piece_refs):
        @pl.when(hop == index)
        def _():
            dyc_ref[...] = piece_ref[...]

    grow = dot(growth_ref[...], expand_ref[...])
    decay = grow[BLOCK - 1 :]
    high, low = split2(dyc_ref[:, :channels].astype(F32) * grow)
    c_t = dyc_ref[:, channels:].T
    later = out_ref[...] * decay
    later_ref[...] = later
    so_far[...] = so_far[...] * decay
    decay_ref[...] = so_far[...]
    out_ref[...] = later + dot(c_t, high) + dot(c_t, low)


def inside_kernel(
    x_ref, b_ref, dy_ref, c_ref, growth_ref, weight_ref, expand_ref,
    inner_ref, grad_inner_ref, grad_b_ref, grad_c_ref, skip_grad_ref,
):
    @pl.when(pl.program_id(0) == 0)
    def _():
        skip_grad_ref[...] = jnp.zeros_like(skip_grad_ref)

    b, c = b_ref[...], c_ref[...]
    x, dy = x_ref[...].astype(F32), dy_ref[...].astype(F32)
    skip_grad_ref[...] += jnp.sum(dy * x, axis=0, keepdims=True)
    x_high, x_low = split2(x * dot(weight_ref[...], expand_ref[...]))
    d_high, d_low = split2(dy * dot(growth_ref[...], expand_ref[...]))
    causal = iota((BLOCK, BLOCK), 0) >= iota((BLOCK, BLOCK), 1)
    anticausal = iota((BLOCK, BLOCK), 0) <= iota((BLOCK, BLOCK), 1)
    k_high, k_low = split2(jnp.where(causal, dot_nt(c, b), 0.0))
    inner_ref[...] = dot(k_high, x_high) + dot(k_high, x_low) + dot(k_low, x_high)
    k_high, k_low = split2(jnp.where(anticausal, dot_nt(b, c), 0.0))
    grad_inner_ref[...] = dot(k_high, d_high) + dot(k_high, d_low) + dot(k_low, d_high)
    mixed = dot_nt(d_high, x_high) + dot_nt(d_high, x_low) + dot_nt(d_low, x_high)
    mixed = jnp.where(causal, mixed, 0.0)
    q_high, q_low = split2(mixed)
    grad_c_ref[...] = dot(q_high, b) + dot(q_low, b)
    q_high, q_low = split2(mixed.T)
    grad_b_ref[...] = dot(q_high, c) + dot(q_low, c)


def forward_kernel(
    x_ref, c_ref, dy_ref, growth_ref, inner_ref, grad_c_ref, before_ref, decay_ref, start_ref,
    skip_ref, expand_ref, collect_ref, own_ref, other_ref, dots_ref,
):
    grow, c = dot(growth_ref[...], expand_ref[...]), c_ref[...]
    grown = dy_ref[...].astype(F32) * grow
    d_high, d_low = split2(grown)
    s_high, s_low = split2(before_ref[...] + decay_ref[...] * start_ref[...])
    inner = inner_ref[...] + dot(c, s_high) + dot(c, s_low)
    grad_c = grad_c_ref[...] + dot_nt(d_high, s_high) + dot_nt(d_high, s_low) + dot_nt(d_low, s_high)
    dots_ref[...] = gather_heads(grown * inner, collect_ref[...])
    y = inner * grow + skip_ref[...] * x_ref[...].astype(F32)
    y, grad_c = y.astype(BF16), grad_c.astype(BF16)
    result = jnp.concatenate([y, grad_c], axis=1)
    core_halves(result[: BLOCK // 2], result[BLOCK // 2 :], own_ref, other_ref)


def backward_kernel(
    x_ref, b_ref, dt_ref, dy_ref, weight_ref, inner_ref, grad_b_ref, later_ref, decay_ref, end_ref,
    state_ref, start_ref, total_ref, dots_ref, rate_ref, skip_ref, expand_ref, collect_ref,
    out_ref, rate_grad_ref, after,
):
    channels, width = x_ref.shape[1], b_ref.shape[1]

    @pl.when(pl.program_id(0) == 0)
    def _():
        final = state_ref[...] + total_ref[...] * start_ref[...]
        meet = jnp.sum(final * end_ref[...], axis=0, keepdims=True)
        after[...] = gather_heads(jnp.broadcast_to(meet, (8, channels)), collect_ref[...])
        rate_grad_ref[...] = jnp.zeros_like(rate_grad_ref)

    b, weigh = b_ref[...], dot(weight_ref[...], expand_ref[...])
    scaled = x_ref[...].astype(F32) * weigh
    x_high, x_low = split2(scaled)
    g_high, g_low = split2(later_ref[...] + decay_ref[...] * end_ref[...])
    inner = inner_ref[...] + dot(b, g_high) + dot(b, g_low)
    pulled = gather_heads(scaled * inner, collect_ref[...])
    out_ref[:, :channels] = (inner * weigh + skip_ref[...] * dy_ref[...].astype(F32)).astype(BF16)
    grad_b = grad_b_ref[...] + dot_nt(x_high, g_high) + dot_nt(x_high, g_low) + dot_nt(x_low, g_high)
    out_ref[:, channels : channels + width] = grad_b.astype(BF16)
    dt = dt_ref[...].astype(F32)
    step, log_decay = step_sizes(dt, rate_ref[...])
    change = dots_ref[...] - pulled
    onward = (iota((BLOCK, BLOCK), 0) <= iota((BLOCK, BLOCK), 1)).astype(BF16)
    grad_log_decay = dot3(onward, change) + after[:1]
    after[...] = after[...] + jnp.sum(change, axis=0, keepdims=True)
    rate_grad_ref[...] += jnp.sum(grad_log_decay * log_decay, axis=0, keepdims=True)
    grad_step = pulled / step - rate_ref[...] * grad_log_decay
    out_ref[:, channels + width :] = (grad_step / (1.0 + jnp.exp(-dt))).astype(BF16)


def scan_kernel(heads, pieces_ref, expand_ref, out_ref, decay_ref):
    count, channels = out_ref.shape[0], out_ref.shape[2]
    decay_ref[...] = dot(three_terms(pieces_ref[:, 0, channels:], heads), expand_ref[...])
    total = jnp.zeros(out_ref.shape[1:], F32)
    for index in range(count):
        out_ref[index] = total
        total = total * decay_ref[index : index + 1] + pieces_ref[index, :, :channels]


def back_scan_kernel(pieces_ref, decay_ref, out_ref):
    total = jnp.zeros(out_ref.shape[1:], F32)
    for index in reversed(range(out_ref.shape[0])):
        out_ref[index] = total
        total = total * decay_ref[index : index + 1] + pieces_ref[index]


def params():
    return pltpu.CompilerParams(vmem_limit_bytes=VMEM_BYTES, dimension_semantics=("arbitrary",))


def cost(flops, traffic):
    return pl.CostEstimate(flops=flops, bytes_accessed=traffic, transcendentals=0)


def seg_exchange(state):
    count = lax.axis_size("seg")
    return lax.all_to_all(state.reshape(count, -1, state.shape[-1]), "seg", 0, 0)


def seg_sum(value):
    count, hop = lax.axis_size("seg"), 1
    while hop < count:
        value = value + lax.ppermute(value, "seg", [(i, i ^ hop) for i in range(count)])
        hop *= 2
    return value


def exchange(value):
    return lax.all_to_all(value, "head", 0, 0)


def swap_cores(own, other):
    count = lax.axis_size("head")
    chips, rows, columns = own.shape
    swapped = lax.ppermute(other, "head", [(i, i ^ 1) for i in range(count)])
    return pl.pallas_call(
        merge_kernel,
        out_shape=[jax.ShapeDtypeStruct((2 * rows, columns), BF16)] * chips,
        compiler_params=pltpu.CompilerParams(vmem_limit_bytes=VMEM_BYTES),
        cost_estimate=cost(rows, 16 * own.size),
    )(own, swapped)


def swap_chips(sent):
    count = lax.axis_size("head")

    def permute(hop, value):
        return lax.ppermute(value, "head", [(i, (i + 2 * hop) % count) for i in range(count)])

    came = {0: sent[0], 1: permute(1, sent[1]), len(sent) - 1: permute(len(sent) - 1, sent[-1])}
    for hop in range(2, len(sent) - 1):
        value, _ = lax.optimization_barrier((sent[hop], list(came.values())[1:]))
        came[hop] = permute(hop, value)
    return [came[hop] for hop in range(len(sent))]


def on_device(inputs, b_rows, c_rows, dt_rows, a_log, d_skip, grad_out):
    shards, segments = lax.axis_size("head"), lax.axis_size("seg")
    rows = inputs.shape[0]
    heads = dt_rows.shape[1] // shards
    channels = inputs.shape[1] // shards
    width = b_rows.shape[1] // shards
    copies = LANES // heads
    first = lax.axis_index("head") * heads
    rate = jnp.exp(a_log)
    rate_here = lax.dynamic_slice_in_dim(rate, first, heads, 0)
    skip_here = lax.dynamic_slice_in_dim(d_skip, first, heads, 0)

    packed_width, pair_width = channels + width + LANES, channels + width
    packed = pl.pallas_call(
        lambda *refs: pack_kernel(heads, *refs),
        grid=(shards // 2,),
        in_specs=[
            pl.BlockSpec((rows, 2 * channels), lambda i: (0, i)),
            pl.BlockSpec((rows, 2 * width), lambda i: (0, i)),
            pl.BlockSpec((rows, LANES), lambda i: (0, 0)),
        ],
        out_specs=pl.BlockSpec((2, rows, packed_width), lambda i: (i, 0, 0)),
        out_shape=jax.ShapeDtypeStruct((shards, rows, packed_width), BF16),
        compiler_params=params(),
        cost_estimate=cost(rows, 4 * shards * rows * packed_width),
    )(inputs, b_rows, dt_rows)
    first_in = exchange(packed)
    half_spec = pl.BlockSpec((None, rows, pair_width), lambda i: (i, 0, 0))
    half_shape = jax.ShapeDtypeStruct((shards // 2, rows, pair_width), BF16)
    own, other = pl.pallas_call(
        pack_pair_kernel,
        grid=(shards // 2,),
        in_specs=[
            pl.BlockSpec((rows, 2 * channels), lambda i: (0, i)),
            pl.BlockSpec((rows, 2 * width), lambda i: (0, i)),
        ],
        out_specs=[half_spec, half_spec],
        out_shape=[half_shape, half_shape],
        compiler_params=params(),
        cost_estimate=cost(rows, 4 * shards * rows * pair_width),
    )(grad_out, c_rows)
    first_in, sent = lax.optimization_barrier((first_in, swap_cores(own, other)))
    second_in = swap_chips(sent)

    length = rows * shards
    blocks = length // BLOCK
    xbd = first_in.reshape(length, packed_width)
    rate_row = jnp.tile(rate_here, copies)[None]
    skip_row = jnp.repeat(skip_here, HEAD_DIM)[None]
    lane, channel = jnp.arange(LANES), jnp.arange(channels)
    same = (lane % heads)[:, None] == (channel // HEAD_DIM)[None, :]
    expand = (same & (lane < 3 * heads)[:, None]).astype(BF16)
    collect = same.T.astype(BF16)

    def whole(array):
        return pl.BlockSpec(array.shape, lambda i: (0,) * array.ndim)

    def sections(place):
        return {
            "main": pl.BlockSpec((BLOCK, channels), lambda i: (place(i), 0)),
            "side": pl.BlockSpec((BLOCK, width), lambda i: (place(i), channels // width)),
            "dt": pl.BlockSpec((BLOCK, LANES), lambda i: (place(i), (channels + width) // LANES)),
            "per_head": pl.BlockSpec((BLOCK, LANES), lambda i: (place(i), 0)),
            "mixed": pl.BlockSpec((BLOCK, BLOCK), lambda i: (place(i), 0)),
            "decay": pl.BlockSpec((None, 1, channels), lambda i: (place(i), 0, 0)),
            "state": pl.BlockSpec((None, width, channels), lambda i: (place(i), 0, 0)),
        }

    onward = sections(lambda i: i)
    back = sections(lambda i: blocks - 1 - i)
    state_shape = jax.ShapeDtypeStruct((width, channels), F32)
    states_shape = jax.ShapeDtypeStruct((blocks, width, channels), F32)
    terms_shape = jax.ShapeDtypeStruct((length, LANES), BF16)
    decays_shape = jax.ShapeDtypeStruct((blocks, 1, channels), F32)
    row_scratch = pltpu.VMEM((1, channels), F32)
    unit = 2 * length * width * channels

    state, growth, weight, before, decay_before = pl.pallas_call(
        lambda *refs: state_kernel(heads, *refs),
        grid=(blocks,),
        in_specs=[
            onward["main"], onward["side"],
            pl.BlockSpec((length, LANES), lambda i: (0, (channels + width) // LANES)),
            whole(rate_row), whole(expand),
        ],
        out_specs=[
            pl.BlockSpec((width, channels + LANES), lambda i: (0, 0)),
            pl.BlockSpec((length, LANES), lambda i: (0, 0)),
            pl.BlockSpec((length, LANES), lambda i: (0, 0)),
            onward["state"], onward["decay"],
        ],
        out_shape=[
            jax.ShapeDtypeStruct((width, channels + LANES), F32),
            terms_shape, terms_shape, states_shape, decays_shape,
        ],
        scratch_shapes=[row_scratch],
        compiler_params=params(),
        cost_estimate=cost(6 * unit, 4 * length * channels),
    )(xbd, xbd, xbd, rate_row, expand)
    piece = (segments, width // segments, channels)
    starts, decays = pl.pallas_call(
        lambda *refs: scan_kernel(heads, *refs),
        out_shape=[jax.ShapeDtypeStruct(piece, F32), jax.ShapeDtypeStruct((segments, channels), F32)],
        compiler_params=pltpu.CompilerParams(vmem_limit_bytes=VMEM_BYTES),
        cost_estimate=cost(unit, 8 * width * channels),
    )(seg_exchange(state), expand)
    starts, _ = lax.optimization_barrier((starts, second_in[1:]))
    start = seg_exchange(starts).reshape(width, channels)

    grad_state, dyc, later, decay_after = pl.pallas_call(
        lambda *refs: grad_state_kernel(len(second_in), *refs),
        grid=(blocks,),
        in_specs=[back["per_head"], whole(expand)] + [whole(part) for part in second_in],
        out_specs=[
            pl.BlockSpec((width, channels), lambda i: (0, 0)),
            pl.BlockSpec((BLOCK, pair_width), lambda i: (blocks - 1 - i, 0)),
            back["state"], back["decay"],
        ],
        out_shape=[
            state_shape, jax.ShapeDtypeStruct((length, pair_width), BF16),
            states_shape, decays_shape,
        ],
        scratch_shapes=[row_scratch],
        compiler_params=params(),
        cost_estimate=cost(6 * unit, 4 * length * channels),
    )(growth, expand, *second_in)
    inner, grad_inner, inside_b, inside_c, skip_grad = pl.pallas_call(
        inside_kernel,
        grid=(blocks,),
        in_specs=[onward[name] for name in ("main", "side", "main", "side", "per_head", "per_head")] + [whole(expand)],
        out_specs=[
            onward["main"], onward["main"], onward["mixed"], onward["mixed"],
            pl.BlockSpec((1, channels), lambda i: (0, 0)),
        ],
        out_shape=[
            jax.ShapeDtypeStruct((length, channels), F32), jax.ShapeDtypeStruct((length, channels), F32),
            jax.ShapeDtypeStruct((length, width), F32), jax.ShapeDtypeStruct((length, width), F32),
            jax.ShapeDtypeStruct((1, channels), F32),
        ],
        compiler_params=params(),
        cost_estimate=cost(12 * unit, 16 * length * channels),
    )(xbd, xbd, dyc, dyc, growth, weight, expand)

    grad_state, _ = lax.optimization_barrier((grad_state, (start, inner)))
    pieces = seg_exchange(grad_state)
    own, other, dots = pl.pallas_call(
        forward_kernel,
        grid=(blocks,),
        in_specs=[
            onward["main"], onward["side"], onward["main"], onward["per_head"],
            onward["main"], onward["mixed"], onward["state"], onward["decay"],
            whole(start), whole(skip_row), whole(expand), whole(collect),
        ],
        out_specs=[half_spec, half_spec, onward["per_head"]],
        out_shape=[half_shape, half_shape, jax.ShapeDtypeStruct((length, LANES), F32)],
        compiler_params=params(),
        cost_estimate=cost(8 * unit, 16 * length * channels),
    )(xbd, dyc, dyc, growth, inner, inside_c, before, decay_before, start, skip_row, expand, collect)
    ends = pl.pallas_call(
        back_scan_kernel,
        out_shape=jax.ShapeDtypeStruct(piece, F32),
        compiler_params=pltpu.CompilerParams(vmem_limit_bytes=VMEM_BYTES),
        cost_estimate=cost(unit, 8 * width * channels),
    )(pieces, decays)
    own, other, _ = lax.optimization_barrier((own, other, pieces))
    first_out = swap_chips(swap_cores(own, other))
    end = seg_exchange(ends).reshape(width, channels)


    total = lax.dynamic_slice_in_dim(decays, lax.axis_index("seg"), 1, 0)
    grads, rate_grad = pl.pallas_call(
        backward_kernel,
        grid=(blocks,),
        in_specs=[
            back["main"], back["side"], back["dt"], back["main"], back["per_head"],
            back["main"], back["mixed"], back["state"], back["decay"],
            whole(end), pl.BlockSpec((width, channels), lambda i: (0, 0)), whole(start), whole(total),
            back["per_head"], whole(rate_row), whole(skip_row), whole(expand), whole(collect),
        ],
        out_specs=[
            pl.BlockSpec((BLOCK, packed_width), lambda i: (blocks - 1 - i, 0)),
            pl.BlockSpec((1, LANES), lambda i: (0, 0)),
        ],
        out_shape=[
            jax.ShapeDtypeStruct((length, packed_width), BF16),
            jax.ShapeDtypeStruct((1, LANES), F32),
        ],
        scratch_shapes=[pltpu.VMEM((8, LANES), F32)],
        compiler_params=params(),
        cost_estimate=cost(8 * unit, 16 * length * channels),
    )(
        xbd, xbd, xbd, dyc, weight, grad_inner, inside_b, later, decay_after,
        end, state, start, total, dots, rate_row, skip_row, expand, collect,
    )
    grads, _ = lax.optimization_barrier((grads, first_out[1:]))
    second_out = exchange(grads.reshape(shards, rows, packed_width))

    skip_grad = skip_grad.reshape(heads, HEAD_DIM).sum(axis=1)
    sums = jnp.concatenate([rate_grad[0, :heads], skip_grad])
    sums = seg_sum(jnp.pad(sums, (0, LANES - 2 * heads))[None])[0]

    grad_x, grad_b, grad_dt = pl.pallas_call(
        lambda *refs: unpack_kernel(heads, *refs),
        grid=(shards // 2,),
        in_specs=[pl.BlockSpec((2, rows, packed_width), lambda i: (i, 0, 0))],
        out_specs=[
            pl.BlockSpec((rows, 2 * channels), lambda i: (0, i)),
            pl.BlockSpec((rows, 2 * width), lambda i: (0, i)),
            pl.BlockSpec((rows, LANES), lambda i: (0, 0)),
        ],
        out_shape=[jax.ShapeDtypeStruct(like.shape, BF16) for like in (inputs, b_rows, dt_rows)],
        compiler_params=params(),
        cost_estimate=cost(rows, 4 * shards * rows * packed_width),
    )(second_out)
    outputs, grad_c = pl.pallas_call(
        lambda *refs: unpack_pairs_kernel(len(first_out), *refs),
        out_shape=[jax.ShapeDtypeStruct(like.shape, BF16) for like in (inputs, c_rows)],
        compiler_params=pltpu.CompilerParams(vmem_limit_bytes=VMEM_BYTES),
        cost_estimate=cost(rows, 4 * shards * rows * pair_width),
    )(*first_out)
    return outputs, grad_x, grad_b, grad_c, grad_dt, sums[:heads], sums[heads : 2 * heads]


def solution(mesh):
    by_rows = P(("dp", "seg", "head"), None)
    in_specs = (by_rows, by_rows, by_rows, by_rows, P(), P(), by_rows)
    out_specs = (by_rows, by_rows, by_rows, by_rows, by_rows, P(("dp", "head")), P(("dp", "head")))
    return jax.shard_map(on_device, mesh=mesh, in_specs=in_specs, out_specs=out_specs, check_vma=False)
```

```python
import jax
import jax.numpy as jnp
from jax import lax
from jax.experimental import pallas as pl
from jax.experimental.pallas import tpu as pltpu
from jax.sharding import PartitionSpec as P

HEAD_DIM = 64
GSTATE = 256
BLOCK = 256
LANES = 128
CHANNELS = 1024
VMEM_BYTES = 50 * 1024 * 1024

F32 = jnp.float32
BF16 = jnp.bfloat16


def dot(left, right):
    return lax.dot_general(left, right, (((1,), (0,)), ((), ())), preferred_element_type=F32)


def dot_nt(left, right):
    return lax.dot_general(left, right, (((1,), (1,)), ((), ())), preferred_element_type=F32)


def split2(value):
    high = value.astype(BF16)
    return high, (value - high.astype(F32)).astype(BF16)


def split3(value):
    high, rest = value.astype(BF16), None
    rest = value - high.astype(F32)
    middle = rest.astype(BF16)
    return high, middle, (rest - middle.astype(F32)).astype(BF16)


def dot3(ones, value):
    high, middle, low = split3(value)
    return dot(ones, high) + dot(ones, middle) + dot(ones, low)


def iota(shape, dim):
    return lax.broadcasted_iota(jnp.int32, shape, dim)


def step_sizes(dt, rate):
    step = jnp.log(1.0 + jnp.exp(dt))
    return step, -step * rate


def three_terms(value, heads):
    high, middle, low = split3(value)
    lane = iota(value.shape, 1)
    return jnp.where(lane < heads, high, jnp.where(lane < 2 * heads, middle, low))


def gather_heads(value, collect):
    high, low = split2(value)
    return dot(high, collect) + dot(low, collect)


def pack_kernel(heads, x_ref, b_ref, dt_ref, out_ref):
    here, channels, width = out_ref.shape[0], CHANNELS, GSTATE
    for index in range(here):
        shard = pl.program_id(0) * here + index
        out_ref[index, :, :channels] = x_ref[:, index * channels : (index + 1) * channels]
        out_ref[index, :, channels : channels + width] = b_ref[:, index * width : (index + 1) * width]
        wanted = shard * heads + lax.rem(iota((LANES, LANES), 1), heads)
        pick = (iota((LANES, LANES), 0) == wanted).astype(BF16)
        out_ref[index, :, channels + width :] = dot(dt_ref[...], pick).astype(BF16)


def unpack_kernel(heads, in_ref, x_ref, b_ref, dt_ref):
    here, channels, width = in_ref.shape[0], CHANNELS, GSTATE
    for index in range(here):
        shard = pl.program_id(0) * here + index
        x_ref[:, index * channels : (index + 1) * channels] = in_ref[index, :, :channels]
        b_ref[:, index * width : (index + 1) * width] = in_ref[index, :, channels : channels + width]
        mine = iota(dt_ref.shape, 1) // heads == shard
        dt_ref[...] = jnp.where(mine, in_ref[index, :, channels + width :], dt_ref[...])


def core_halves(first, second, own_ref, other_ref):
    core = lax.rem(lax.axis_index("head"), 2)

    @pl.when(core == 0)
    def _():
        own_ref[...], other_ref[...] = first, second

    @pl.when(core == 1)
    def _():
        own_ref[...], other_ref[...] = second, first


def pack_pair_kernel(dy_ref, c_ref, own_ref, other_ref):
    channels, width = CHANNELS, GSTATE
    first = jnp.concatenate([dy_ref[:, :channels], c_ref[:, :width]], axis=1)
    second = jnp.concatenate([dy_ref[:, channels:], c_ref[:, width:]], axis=1)
    core_halves(first, second, own_ref, other_ref)


def merge_kernel(own_ref, swapped_ref, *out_refs):
    me, chips, rows = lax.axis_index("head"), own_ref.shape[0], own_ref.shape[1]
    core = lax.rem(me, 2)
    for hop, out_ref in enumerate(out_refs):
        chip = lax.rem(me // 2 + hop, chips)
        out_ref[pl.ds(pl.multiple_of(core * rows, rows), rows), :] = own_ref[chip]
        out_ref[pl.ds(pl.multiple_of((1 - core) * rows, rows), rows), :] = swapped_ref[chip]


def unpack_pairs_kernel(pieces, *refs):
    piece_refs, (y_ref, c_ref) = refs[:pieces], refs[pieces:]
    me, rows, channels, width = lax.axis_index("head"), y_ref.shape[0], CHANNELS, GSTATE
    for hop, piece_ref in enumerate(piece_refs):
        chip = lax.rem(me // 2 - hop + pieces, pieces)
        for core in range(2):
            part = slice(core * rows, (core + 1) * rows)
            at = pl.multiple_of((2 * chip + core) * channels, channels)
            y_ref[:, pl.ds(at, channels)] = piece_ref[part, :channels]
            at = pl.multiple_of((2 * chip + core) * width, width)
            c_ref[:, pl.ds(at, width)] = piece_ref[part, channels:]


def state_kernel(
    heads, x_ref, b_ref, dt_ref, rate_ref, expand_ref,
    out_ref, growth_ref, weight_ref, high_ref, low_ref, before_ref, decay_ref, so_far,
):
    block = pl.program_id(0)
    channels = x_ref.shape[1]

    @pl.when(block == 0)
    def _():
        out_ref[...] = jnp.zeros_like(out_ref)
        so_far[...] = jnp.ones_like(so_far)
        lower = (iota((BLOCK, BLOCK), 0) >= iota((BLOCK, BLOCK), 1)).astype(BF16)
        log_total = jnp.zeros((1, LANES), F32)
        for at in range(0, dt_ref.shape[0], BLOCK):
            rows = slice(at, at + BLOCK)
            step, log_decay = step_sizes(dt_ref[rows].astype(F32), rate_ref[...])
            cumulative = dot3(lower, log_decay)
            growth_ref[rows] = three_terms(jnp.exp(cumulative), heads)
            weight_ref[rows] = three_terms(jnp.exp(-cumulative) * step, heads)
            log_total = log_total + cumulative[BLOCK - 1 :]
        out_ref[:, channels:] = jnp.broadcast_to(jnp.exp(log_total), (out_ref.shape[0], LANES))

    rows = pl.ds(pl.multiple_of(block * BLOCK, BLOCK), BLOCK)
    ends = pl.ds(pl.multiple_of(block * BLOCK + BLOCK - 16, 16), 16)
    spread = expand_ref[...]
    high, low = split2(x_ref[...].astype(F32) * dot(weight_ref[rows, :], spread))
    high_ref[...], low_ref[...] = high, low
    decay = dot(growth_ref[ends, :], spread)[15:]
    b_t = b_ref[...].T
    state = out_ref[:, :channels]
    before_ref[...] = state
    decay_ref[...] = so_far[...]
    so_far[...] = so_far[...] * decay
    out_ref[:, :channels] = (state + dot(b_t, high) + dot(b_t, low)) * decay


def grad_state_kernel(pieces, growth_ref, expand_ref, *refs):
    piece_refs, (out_ref, dyc_ref, high_ref, low_ref, later_ref, decay_ref, so_far) = refs[:pieces], refs[pieces:]
    channels = out_ref.shape[1]
    block = pl.num_programs(0) - 1 - pl.program_id(0)
    hop = lax.rem(lax.axis_index("head") // 2 - block + pieces, pieces)

    @pl.when(pl.program_id(0) == 0)
    def _():
        out_ref[...] = jnp.zeros_like(out_ref)
        so_far[...] = jnp.ones_like(so_far)

    for index, piece_ref in enumerate(piece_refs):
        @pl.when(hop == index)
        def _():
            dyc_ref[...] = piece_ref[...]

    grow = dot(growth_ref[...], expand_ref[...])
    decay = grow[BLOCK - 1 :]
    high, low = split2(dyc_ref[:, :channels].astype(F32) * grow)
    high_ref[...], low_ref[...] = high, low
    c_t = dyc_ref[:, channels:].T
    later = out_ref[...] * decay
    later_ref[...] = later
    so_far[...] = so_far[...] * decay
    decay_ref[...] = so_far[...]
    out_ref[...] = later + dot(c_t, high) + dot(c_t, low)


def inside_kernel(
    x_ref, x_high_ref, x_low_ref, b_ref, dy_ref, d_high_ref, d_low_ref, c_ref,
    inner_ref, grad_b_ref, grad_c_ref, skip_grad_ref,
):
    @pl.when(pl.program_id(0) == 0)
    def _():
        skip_grad_ref[...] = jnp.zeros_like(skip_grad_ref)

    b, c = b_ref[...], c_ref[...]
    skip_grad_ref[...] += jnp.sum(dy_ref[...].astype(F32) * x_ref[...].astype(F32), axis=0, keepdims=True)
    x_high, x_low, d_high, d_low = x_high_ref[...], x_low_ref[...], d_high_ref[...], d_low_ref[...]
    causal = iota((BLOCK, BLOCK), 0) >= iota((BLOCK, BLOCK), 1)
    k_high, k_low = split2(jnp.where(causal, dot_nt(c, b), 0.0))
    inner_ref[...] = dot(k_high, x_high) + dot(k_high, x_low) + dot(k_low, x_high)
    mixed = dot_nt(d_high, x_high) + dot_nt(d_high, x_low) + dot_nt(d_low, x_high)
    mixed = jnp.where(causal, mixed, 0.0)
    q_high, q_low = split2(mixed)
    grad_c_ref[...] = dot(q_high, b) + dot(q_low, b)
    q_high, q_low = split2(mixed.T)
    grad_b_ref[...] = dot(q_high, c) + dot(q_low, c)


def inside_grad_kernel(b_ref, d_high_ref, d_low_ref, c_ref, state_ref, start_ref, total_ref, out_ref, final_ref):
    final_ref[...] = state_ref[...] + total_ref[...] * start_ref[...]
    d_high, d_low = d_high_ref[...], d_low_ref[...]
    anticausal = iota((BLOCK, BLOCK), 0) <= iota((BLOCK, BLOCK), 1)
    k_high, k_low = split2(jnp.where(anticausal, dot_nt(b_ref[...], c_ref[...]), 0.0))
    out_ref[...] = dot(k_high, d_high) + dot(k_high, d_low) + dot(k_low, d_high)


def forward_kernel(
    x_ref, c_ref, dy_ref, growth_ref, inner_ref, grad_c_ref, before_ref, decay_ref, start_ref,
    skip_ref, expand_ref, collect_ref, own_ref, other_ref, dots_ref,
):
    grow, c = dot(growth_ref[...], expand_ref[...]), c_ref[...]
    grown = dy_ref[...].astype(F32) * grow
    d_high, d_low = split2(grown)
    s_high, s_low = split2(before_ref[...] + decay_ref[...] * start_ref[...])
    inner = inner_ref[...] + dot(c, s_high) + dot(c, s_low)
    grad_c = grad_c_ref[...] + dot_nt(d_high, s_high) + dot_nt(d_high, s_low) + dot_nt(d_low, s_high)
    dots_ref[...] = gather_heads(grown * inner, collect_ref[...])
    y = inner * grow + skip_ref[...] * x_ref[...].astype(F32)
    y, grad_c = y.astype(BF16), grad_c.astype(BF16)
    result = jnp.concatenate([y, grad_c], axis=1)
    core_halves(result[: BLOCK // 2], result[BLOCK // 2 :], own_ref, other_ref)


def backward_kernel(
    x_ref, b_ref, dt_ref, dy_ref, weight_ref, inner_ref, grad_b_ref, later_ref, decay_ref, end_ref,
    final_ref, dots_ref, rate_ref, skip_ref, expand_ref, collect_ref,
    out_ref, rate_grad_ref, after,
):
    channels, width = x_ref.shape[1], b_ref.shape[1]

    @pl.when(pl.program_id(0) == 0)
    def _():
        meet = jnp.sum(final_ref[...] * end_ref[...], axis=0, keepdims=True)
        after[...] = gather_heads(jnp.broadcast_to(meet, (8, channels)), collect_ref[...])
        rate_grad_ref[...] = jnp.zeros_like(rate_grad_ref)

    b, weigh = b_ref[...], dot(weight_ref[...], expand_ref[...])
    scaled = x_ref[...].astype(F32) * weigh
    x_high, x_low = split2(scaled)
    g_high, g_low = split2(later_ref[...] + decay_ref[...] * end_ref[...])
    inner = inner_ref[...] + dot(b, g_high) + dot(b, g_low)
    pulled = gather_heads(scaled * inner, collect_ref[...])
    out_ref[:, :channels] = (inner * weigh + skip_ref[...] * dy_ref[...].astype(F32)).astype(BF16)
    grad_b = grad_b_ref[...] + dot_nt(x_high, g_high) + dot_nt(x_high, g_low) + dot_nt(x_low, g_high)
    out_ref[:, channels : channels + width] = grad_b.astype(BF16)
    dt = dt_ref[...].astype(F32)
    step, log_decay = step_sizes(dt, rate_ref[...])
    change = dots_ref[...] - pulled
    onward = (iota((BLOCK, BLOCK), 0) <= iota((BLOCK, BLOCK), 1)).astype(BF16)
    grad_log_decay = dot3(onward, change) + after[:1]
    after[...] = after[...] + jnp.sum(change, axis=0, keepdims=True)
    rate_grad_ref[...] += jnp.sum(grad_log_decay * log_decay, axis=0, keepdims=True)
    grad_step = pulled / step - rate_ref[...] * grad_log_decay
    out_ref[:, channels + width :] = (grad_step / (1.0 + jnp.exp(-dt))).astype(BF16)


def scan_kernel(heads, pieces_ref, expand_ref, out_ref, decay_ref):
    count, channels = out_ref.shape[0], out_ref.shape[2]
    decay_ref[...] = dot(three_terms(pieces_ref[:, 0, channels:], heads), expand_ref[...])
    total = jnp.zeros(out_ref.shape[1:], F32)
    for index in range(count):
        out_ref[index] = total
        total = total * decay_ref[index : index + 1] + pieces_ref[index, :, :channels]


def back_scan_kernel(pieces_ref, decay_ref, out_ref):
    total = jnp.zeros(out_ref.shape[1:], F32)
    for index in reversed(range(out_ref.shape[0])):
        out_ref[index] = total
        total = total * decay_ref[index : index + 1] + pieces_ref[index]


def params(mebibytes=VMEM_BYTES >> 20):
    return pltpu.CompilerParams(vmem_limit_bytes=mebibytes << 20, dimension_semantics=("arbitrary",))


def cost(flops, traffic):
    return pl.CostEstimate(flops=flops, bytes_accessed=traffic, transcendentals=0)


def seg_exchange(state):
    count = lax.axis_size("seg")
    return lax.all_to_all(state.reshape(count, -1, state.shape[-1]), "seg", 0, 0)


def seg_sum(value):
    count, hop = lax.axis_size("seg"), 1
    while hop < count:
        value = value + lax.ppermute(value, "seg", [(i, i ^ hop) for i in range(count)])
        hop *= 2
    return value


def exchange(value):
    return lax.all_to_all(value, "head", 0, 0)


def swap_cores(own, other):
    count = lax.axis_size("head")
    chips, rows, columns = own.shape
    swapped = lax.ppermute(other, "head", [(i, i ^ 1) for i in range(count)])
    return pl.pallas_call(
        merge_kernel,
        out_shape=[jax.ShapeDtypeStruct((2 * rows, columns), BF16)] * chips,
        compiler_params=pltpu.CompilerParams(vmem_limit_bytes=VMEM_BYTES),
        cost_estimate=cost(rows, 16 * own.size),
    )(own, swapped)


def swap_chips(sent, between):
    count = lax.axis_size("head")

    def permute(hop, value):
        return lax.ppermute(value, "head", [(i, (i + 2 * hop) % count) for i in range(count)])

    came = {0: sent[0], 1: permute(1, sent[1]), len(sent) - 1: permute(len(sent) - 1, sent[-1])}
    for hop in range(2, len(sent) - 1):
        value, *_ = lax.optimization_barrier((sent[hop], list(came.values())[1:], between))
        came[hop] = permute(hop, value)
    return [came[hop] for hop in range(len(sent))]


def on_device(inputs, b_rows, c_rows, dt_rows, a_log, d_skip, grad_out):
    shards, segments = lax.axis_size("head"), lax.axis_size("seg")
    rows = inputs.shape[0]
    heads = dt_rows.shape[1] // shards
    channels = inputs.shape[1] // shards
    width = b_rows.shape[1] // shards
    copies = LANES // heads
    first = lax.axis_index("head") * heads
    rate = jnp.exp(a_log)
    rate_here = lax.dynamic_slice_in_dim(rate, first, heads, 0)
    skip_here = lax.dynamic_slice_in_dim(d_skip, first, heads, 0)

    packed_width, pair_width = channels + width + LANES, channels + width
    packed = pl.pallas_call(
        lambda *refs: pack_kernel(heads, *refs),
        grid=(shards // 4,),
        in_specs=[
            pl.BlockSpec((rows, 4 * channels), lambda i: (0, i)),
            pl.BlockSpec((rows, 4 * width), lambda i: (0, i)),
            pl.BlockSpec((rows, LANES), lambda i: (0, 0)),
        ],
        out_specs=pl.BlockSpec((4, rows, packed_width), lambda i: (i, 0, 0)),
        out_shape=jax.ShapeDtypeStruct((shards, rows, packed_width), BF16),
        compiler_params=params(61),
        cost_estimate=cost(rows, 4 * shards * rows * packed_width),
    )(inputs, b_rows, dt_rows)
    first_in = exchange(packed)
    half_spec = pl.BlockSpec((None, rows, pair_width), lambda i: (i, 0, 0))
    half_shape = jax.ShapeDtypeStruct((shards // 2, rows, pair_width), BF16)
    own, other = pl.pallas_call(
        pack_pair_kernel,
        grid=(shards // 2,),
        in_specs=[
            pl.BlockSpec((rows, 2 * channels), lambda i: (0, i)),
            pl.BlockSpec((rows, 2 * width), lambda i: (0, i)),
        ],
        out_specs=[half_spec, half_spec],
        out_shape=[half_shape, half_shape],
        compiler_params=params(),
        cost_estimate=cost(rows, 4 * shards * rows * pair_width),
    )(grad_out, c_rows)
    first_in, sent = lax.optimization_barrier((first_in, swap_cores(own, other)))
    second_in = swap_chips(sent, None)

    length = rows * shards
    blocks = length // BLOCK
    xbd = first_in.reshape(length, packed_width)
    rate_row = jnp.tile(rate_here, copies)[None]
    skip_row = jnp.repeat(skip_here, HEAD_DIM)[None]
    lane, channel = jnp.arange(LANES), jnp.arange(channels)
    same = (lane % heads)[:, None] == (channel // HEAD_DIM)[None, :]
    expand = (same & (lane < 3 * heads)[:, None]).astype(BF16)
    collect = same.T.astype(BF16)

    def whole(array):
        return pl.BlockSpec(array.shape, lambda i: (0,) * array.ndim)

    def sections(place):
        return {
            "main": pl.BlockSpec((BLOCK, channels), lambda i: (place(i), 0)),
            "side": pl.BlockSpec((BLOCK, width), lambda i: (place(i), channels // width)),
            "dt": pl.BlockSpec((BLOCK, LANES), lambda i: (place(i), (channels + width) // LANES)),
            "per_head": pl.BlockSpec((BLOCK, LANES), lambda i: (place(i), 0)),
            "mixed": pl.BlockSpec((BLOCK, BLOCK), lambda i: (place(i), 0)),
            "decay": pl.BlockSpec((None, 1, channels), lambda i: (place(i), 0, 0)),
            "state": pl.BlockSpec((None, width, channels), lambda i: (place(i), 0, 0)),
        }

    onward = sections(lambda i: i)
    back = sections(lambda i: blocks - 1 - i)
    state_shape = jax.ShapeDtypeStruct((width, channels), F32)
    states_shape = jax.ShapeDtypeStruct((blocks, width, channels), F32)
    terms_shape = jax.ShapeDtypeStruct((length, LANES), BF16)
    main_shape = jax.ShapeDtypeStruct((length, channels), BF16)
    decays_shape = jax.ShapeDtypeStruct((blocks, 1, channels), F32)
    row_scratch = pltpu.VMEM((1, channels), F32)
    unit = 2 * length * width * channels

    state, growth, weight, x_high, x_low, before, decay_before = pl.pallas_call(
        lambda *refs: state_kernel(heads, *refs),
        grid=(blocks,),
        in_specs=[
            onward["main"], onward["side"],
            pl.BlockSpec((length, LANES), lambda i: (0, (channels + width) // LANES)),
            whole(rate_row), whole(expand),
        ],
        out_specs=[
            pl.BlockSpec((width, channels + LANES), lambda i: (0, 0)),
            pl.BlockSpec((length, LANES), lambda i: (0, 0)),
            pl.BlockSpec((length, LANES), lambda i: (0, 0)),
            onward["main"], onward["main"], onward["state"], onward["decay"],
        ],
        out_shape=[
            jax.ShapeDtypeStruct((width, channels + LANES), F32),
            terms_shape, terms_shape, main_shape, main_shape, states_shape, decays_shape,
        ],
        scratch_shapes=[row_scratch],
        compiler_params=params(),
        cost_estimate=cost(6 * unit, 4 * length * channels),
    )(xbd, xbd, xbd, rate_row, expand)
    piece = (segments, width // segments, channels)
    starts, decays = pl.pallas_call(
        lambda *refs: scan_kernel(heads, *refs),
        out_shape=[jax.ShapeDtypeStruct(piece, F32), jax.ShapeDtypeStruct((segments, channels), F32)],
        compiler_params=pltpu.CompilerParams(vmem_limit_bytes=VMEM_BYTES),
        cost_estimate=cost(unit, 8 * width * channels),
    )(seg_exchange(state), expand)
    starts, _ = lax.optimization_barrier((starts, second_in[1:]))
    start = seg_exchange(starts).reshape(width, channels)

    grad_state, dyc, d_high, d_low, later, decay_after = pl.pallas_call(
        lambda *refs: grad_state_kernel(len(second_in), *refs),
        grid=(blocks,),
        in_specs=[back["per_head"], whole(expand)] + [whole(part) for part in second_in],
        out_specs=[
            pl.BlockSpec((width, channels), lambda i: (0, 0)),
            pl.BlockSpec((BLOCK, pair_width), lambda i: (blocks - 1 - i, 0)),
            back["main"], back["main"], back["state"], back["decay"],
        ],
        out_shape=[
            state_shape, jax.ShapeDtypeStruct((length, pair_width), BF16),
            main_shape, main_shape, states_shape, decays_shape,
        ],
        scratch_shapes=[row_scratch],
        compiler_params=params(),
        cost_estimate=cost(6 * unit, 4 * length * channels),
    )(growth, expand, *second_in)
    inner, inside_b, inside_c, skip_grad = pl.pallas_call(
        inside_kernel,
        grid=(blocks,),
        in_specs=[onward[name] for name in ("main", "main", "main", "side", "main", "main", "main", "side")],
        out_specs=[
            onward["main"], onward["mixed"], onward["mixed"],
            pl.BlockSpec((1, channels), lambda i: (0, 0)),
        ],
        out_shape=[
            jax.ShapeDtypeStruct((length, channels), F32),
            jax.ShapeDtypeStruct((length, width), F32), jax.ShapeDtypeStruct((length, width), F32),
            jax.ShapeDtypeStruct((1, channels), F32),
        ],
        compiler_params=params(),
        cost_estimate=cost(8 * unit, 16 * length * channels),
    )(xbd, x_high, x_low, xbd, dyc, d_high, d_low, dyc)

    grad_state, _ = lax.optimization_barrier((grad_state, (start, inner)))
    pieces = seg_exchange(grad_state)
    own, other, dots = pl.pallas_call(
        forward_kernel,
        grid=(blocks,),
        in_specs=[
            onward["main"], onward["side"], onward["main"], onward["per_head"],
            onward["main"], onward["mixed"], onward["state"], onward["decay"],
            whole(start), whole(skip_row), whole(expand), whole(collect),
        ],
        out_specs=[half_spec, half_spec, onward["per_head"]],
        out_shape=[half_shape, half_shape, jax.ShapeDtypeStruct((length, LANES), F32)],
        compiler_params=params(),
        cost_estimate=cost(8 * unit, 16 * length * channels),
    )(xbd, dyc, dyc, growth, inner, inside_c, before, decay_before, start, skip_row, expand, collect)
    ends = pl.pallas_call(
        back_scan_kernel,
        out_shape=jax.ShapeDtypeStruct(piece, F32),
        compiler_params=pltpu.CompilerParams(vmem_limit_bytes=VMEM_BYTES),
        cost_estimate=cost(unit, 8 * width * channels),
    )(pieces, decays)
    own, other, _ = lax.optimization_barrier((own, other, pieces))
    d_high, _ = lax.optimization_barrier((d_high, pieces))
    total = lax.dynamic_slice_in_dim(decays, lax.axis_index("seg"), 1, 0)
    slab = pl.BlockSpec((width // blocks, channels), lambda i: (i, 0))
    grad_inner, final = pl.pallas_call(
        inside_grad_kernel,
        grid=(blocks,),
        in_specs=[onward[name] for name in ("side", "main", "main", "side")] + [slab, slab, whole(total)],
        out_specs=[onward["main"], slab],
        out_shape=[jax.ShapeDtypeStruct((length, channels), F32), state_shape],
        compiler_params=params(),
        cost_estimate=cost(4 * unit, 8 * length * channels),
    )(xbd, d_high, d_low, dyc, state, start, total)
    first_out = swap_chips(swap_cores(own, other), grad_inner)
    end = seg_exchange(ends).reshape(width, channels)


    grads, rate_grad = pl.pallas_call(
        backward_kernel,
        grid=(blocks,),
        in_specs=[
            back["main"], back["side"], back["dt"], back["main"], back["per_head"],
            back["main"], back["mixed"], back["state"], back["decay"],
            whole(end), whole(final),
            back["per_head"], whole(rate_row), whole(skip_row), whole(expand), whole(collect),
        ],
        out_specs=[
            pl.BlockSpec((BLOCK, packed_width), lambda i: (blocks - 1 - i, 0)),
            pl.BlockSpec((1, LANES), lambda i: (0, 0)),
        ],
        out_shape=[
            jax.ShapeDtypeStruct((length, packed_width), BF16),
            jax.ShapeDtypeStruct((1, LANES), F32),
        ],
        scratch_shapes=[pltpu.VMEM((8, LANES), F32)],
        compiler_params=params(),
        cost_estimate=cost(8 * unit, 16 * length * channels),
    )(
        xbd, xbd, xbd, dyc, weight, grad_inner, inside_b, later, decay_after,
        end, final, dots, rate_row, skip_row, expand, collect,
    )
    grads, _ = lax.optimization_barrier((grads, first_out[1:]))
    second_out = exchange(grads.reshape(shards, rows, packed_width))

    skip_grad = skip_grad.reshape(heads, HEAD_DIM).sum(axis=1)
    sums = jnp.concatenate([rate_grad[0, :heads], skip_grad])
    sums = seg_sum(jnp.pad(sums, (0, LANES - 2 * heads))[None])[0]

    grad_x, grad_b, grad_dt = pl.pallas_call(
        lambda *refs: unpack_kernel(heads, *refs),
        grid=(shards // 2,),
        in_specs=[pl.BlockSpec((2, rows, packed_width), lambda i: (i, 0, 0))],
        out_specs=[
            pl.BlockSpec((rows, 2 * channels), lambda i: (0, i)),
            pl.BlockSpec((rows, 2 * width), lambda i: (0, i)),
            pl.BlockSpec((rows, LANES), lambda i: (0, 0)),
        ],
        out_shape=[jax.ShapeDtypeStruct(like.shape, BF16) for like in (inputs, b_rows, dt_rows)],
        compiler_params=params(),
        cost_estimate=cost(rows, 4 * shards * rows * packed_width),
    )(second_out)
    outputs, grad_c = pl.pallas_call(
        lambda *refs: unpack_pairs_kernel(len(first_out), *refs),
        out_shape=[jax.ShapeDtypeStruct(like.shape, BF16) for like in (inputs, c_rows)],
        compiler_params=pltpu.CompilerParams(vmem_limit_bytes=VMEM_BYTES),
        cost_estimate=cost(rows, 4 * shards * rows * pair_width),
    )(*first_out)
    return outputs, grad_x, grad_b, grad_c, grad_dt, sums[:heads], sums[heads : 2 * heads]


def solution(mesh):
    by_rows = P(("dp", "seg", "head"), None)
    in_specs = (by_rows, by_rows, by_rows, by_rows, P(), P(), by_rows)
    out_specs = (by_rows, by_rows, by_rows, by_rows, by_rows, P(("dp", "head")), P(("dp", "head")))
    return jax.shard_map(on_device, mesh=mesh, in_specs=in_specs, out_specs=out_specs, check_vma=False)
```

```python
import jax
import jax.numpy as jnp
from jax import lax
from jax.experimental import pallas as pl
from jax.experimental.pallas import tpu as pltpu
from jax.sharding import PartitionSpec as P

HEAD_DIM = 64
GSTATE = 256
BLOCK = 256
LANES = 128
CHANNELS = 1024
VMEM_BYTES = 50 * 1024 * 1024

F32 = jnp.float32
BF16 = jnp.bfloat16


def dot(left, right):
    return lax.dot_general(left, right, (((1,), (0,)), ((), ())), preferred_element_type=F32)


def dot_nt(left, right):
    return lax.dot_general(left, right, (((1,), (1,)), ((), ())), preferred_element_type=F32)


def split2(value):
    high = value.astype(BF16)
    return high, (value - high.astype(F32)).astype(BF16)


def split3(value):
    high, rest = value.astype(BF16), None
    rest = value - high.astype(F32)
    middle = rest.astype(BF16)
    return high, middle, (rest - middle.astype(F32)).astype(BF16)


def dot3(ones, value):
    high, middle, low = split3(value)
    return dot(ones, high) + dot(ones, middle) + dot(ones, low)


def iota(shape, dim):
    return lax.broadcasted_iota(jnp.int32, shape, dim)


def step_sizes(dt, rate):
    step = jnp.log(1.0 + jnp.exp(dt))
    return step, -step * rate


def three_terms(value, heads):
    high, middle, low = split3(value)
    lane = iota(value.shape, 1)
    return jnp.where(lane < heads, high, jnp.where(lane < 2 * heads, middle, low))


def gather_heads(value, collect):
    high, low = split2(value)
    return dot(high, collect) + dot(low, collect)


def pack_kernel(heads, x_ref, b_ref, dt_ref, out_ref):
    here, channels, width = out_ref.shape[0], CHANNELS, GSTATE
    for index in range(here):
        shard = pl.program_id(0) * here + index
        out_ref[index, :, :channels] = x_ref[:, index * channels : (index + 1) * channels]
        out_ref[index, :, channels : channels + width] = b_ref[:, index * width : (index + 1) * width]
        wanted = shard * heads + lax.rem(iota((LANES, LANES), 1), heads)
        pick = (iota((LANES, LANES), 0) == wanted).astype(BF16)
        out_ref[index, :, channels + width :] = dot(dt_ref[...], pick).astype(BF16)


def unpack_kernel(heads, in_ref, x_ref, b_ref, dt_ref):
    here, channels, width = in_ref.shape[0], CHANNELS, GSTATE
    for index in range(here):
        shard = pl.program_id(0) * here + index
        x_ref[:, index * channels : (index + 1) * channels] = in_ref[index, :, :channels]
        b_ref[:, index * width : (index + 1) * width] = in_ref[index, :, channels : channels + width]
        mine = iota(dt_ref.shape, 1) // heads == shard
        dt_ref[...] = jnp.where(mine, in_ref[index, :, channels + width :], dt_ref[...])


def core_halves(first, second, own_ref, other_ref):
    core = lax.rem(lax.axis_index("head"), 2)

    @pl.when(core == 0)
    def _():
        own_ref[...], other_ref[...] = first, second

    @pl.when(core == 1)
    def _():
        own_ref[...], other_ref[...] = second, first


def pack_pair_kernel(dy_ref, c_ref, own_ref, other_ref):
    channels, width = CHANNELS, GSTATE
    first = jnp.concatenate([dy_ref[:, :channels], c_ref[:, :width]], axis=1)
    second = jnp.concatenate([dy_ref[:, channels:], c_ref[:, width:]], axis=1)
    core_halves(first, second, own_ref, other_ref)


def merge_kernel(own_ref, swapped_ref, *out_refs):
    me, chips, rows = lax.axis_index("head"), own_ref.shape[0], own_ref.shape[1]
    core = lax.rem(me, 2)
    for hop, out_ref in enumerate(out_refs):
        chip = lax.rem(me // 2 + hop, chips)
        out_ref[pl.ds(pl.multiple_of(core * rows, rows), rows), :] = own_ref[chip]
        out_ref[pl.ds(pl.multiple_of((1 - core) * rows, rows), rows), :] = swapped_ref[chip]


def unpack_pairs_kernel(pieces, *refs):
    piece_refs, (y_ref, c_ref) = refs[:pieces], refs[pieces:]
    me, rows, channels, width = lax.axis_index("head"), y_ref.shape[0], CHANNELS, GSTATE
    for hop, piece_ref in enumerate(piece_refs):
        chip = lax.rem(me // 2 - hop + pieces, pieces)
        for core in range(2):
            part = slice(core * rows, (core + 1) * rows)
            at = pl.multiple_of((2 * chip + core) * channels, channels)
            y_ref[:, pl.ds(at, channels)] = piece_ref[part, :channels]
            at = pl.multiple_of((2 * chip + core) * width, width)
            c_ref[:, pl.ds(at, width)] = piece_ref[part, channels:]


def state_kernel(
    heads, x_ref, b_ref, dt_ref, rate_ref, expand_ref,
    out_ref, growth_ref, weight_ref, high_ref, low_ref, before_ref, decay_ref, so_far,
):
    block = pl.program_id(0)
    channels = x_ref.shape[1]

    @pl.when(block == 0)
    def _():
        out_ref[...] = jnp.zeros_like(out_ref)
        so_far[...] = jnp.ones_like(so_far)
        lower = (iota((BLOCK, BLOCK), 0) >= iota((BLOCK, BLOCK), 1)).astype(BF16)
        log_total = jnp.zeros((1, LANES), F32)
        for at in range(0, dt_ref.shape[0], BLOCK):
            rows = slice(at, at + BLOCK)
            step, log_decay = step_sizes(dt_ref[rows].astype(F32), rate_ref[...])
            cumulative = dot3(lower, log_decay)
            growth_ref[rows] = three_terms(jnp.exp(cumulative), heads)
            weight_ref[rows] = three_terms(jnp.exp(-cumulative) * step, heads)
            log_total = log_total + cumulative[BLOCK - 1 :]
        out_ref[:, channels:] = jnp.broadcast_to(jnp.exp(log_total), (out_ref.shape[0], LANES))

    rows = pl.ds(pl.multiple_of(block * BLOCK, BLOCK), BLOCK)
    ends = pl.ds(pl.multiple_of(block * BLOCK + BLOCK - 16, 16), 16)
    spread = expand_ref[...]
    high, low = split2(x_ref[...].astype(F32) * dot(weight_ref[rows, :], spread))
    high_ref[...], low_ref[...] = high, low
    decay = dot(growth_ref[ends, :], spread)[15:]
    b_t = b_ref[...].T
    state = out_ref[:, :channels]
    before_ref[...] = state
    decay_ref[...] = so_far[...]
    so_far[...] = so_far[...] * decay
    out_ref[:, :channels] = (state + dot(b_t, high) + dot(b_t, low)) * decay


def grad_state_kernel(pieces, growth_ref, expand_ref, *refs):
    piece_refs, (out_ref, dyc_ref, high_ref, low_ref, later_ref, decay_ref, so_far) = refs[:pieces], refs[pieces:]
    channels = out_ref.shape[1]
    block = pl.num_programs(0) - 1 - pl.program_id(0)
    hop = lax.rem(lax.axis_index("head") // 2 - block + pieces, pieces)

    @pl.when(pl.program_id(0) == 0)
    def _():
        out_ref[...] = jnp.zeros_like(out_ref)
        so_far[...] = jnp.ones_like(so_far)

    for index, piece_ref in enumerate(piece_refs):
        @pl.when(hop == index)
        def _():
            dyc_ref[...] = piece_ref[...]

    grow = dot(growth_ref[...], expand_ref[...])
    decay = grow[BLOCK - 1 :]
    high, low = split2(dyc_ref[:, :channels].astype(F32) * grow)
    high_ref[...], low_ref[...] = high, low
    c_t = dyc_ref[:, channels:].T
    later = out_ref[...] * decay
    later_ref[...] = later
    so_far[...] = so_far[...] * decay
    decay_ref[...] = so_far[...]
    out_ref[...] = later + dot(c_t, high) + dot(c_t, low)


def inside_kernel(
    x_ref, x_high_ref, x_low_ref, b_ref, dy_ref, d_high_ref, d_low_ref, c_ref,
    inner_ref, grad_b_ref, grad_c_ref, skip_grad_ref,
):
    @pl.when(pl.program_id(0) == 0)
    def _():
        skip_grad_ref[...] = jnp.zeros_like(skip_grad_ref)

    b, c = b_ref[...], c_ref[...]
    skip_grad_ref[...] += jnp.sum(dy_ref[...].astype(F32) * x_ref[...].astype(F32), axis=0, keepdims=True)
    x_high, x_low, d_high, d_low = x_high_ref[...], x_low_ref[...], d_high_ref[...], d_low_ref[...]
    causal = iota((BLOCK, BLOCK), 0) >= iota((BLOCK, BLOCK), 1)
    k_high, k_low = split2(jnp.where(causal, dot_nt(c, b), 0.0))
    inner_ref[...] = dot(k_high, x_high) + dot(k_high, x_low) + dot(k_low, x_high)
    mixed = dot_nt(d_high, x_high) + dot_nt(d_high, x_low) + dot_nt(d_low, x_high)
    mixed = jnp.where(causal, mixed, 0.0)
    q_high, q_low = split2(mixed)
    grad_c_ref[...] = dot(q_high, b) + dot(q_low, b)
    q_high, q_low = split2(mixed.T)
    grad_b_ref[...] = dot(q_high, c) + dot(q_low, c)


def inside_grad_kernel(b_ref, d_high_ref, d_low_ref, c_ref, state_ref, start_ref, total_ref, out_ref, final_ref):
    final_ref[...] = state_ref[...] + total_ref[...] * start_ref[...]
    d_high, d_low = d_high_ref[...], d_low_ref[...]
    anticausal = iota((BLOCK, BLOCK), 0) <= iota((BLOCK, BLOCK), 1)
    k_high, k_low = split2(jnp.where(anticausal, dot_nt(b_ref[...], c_ref[...]), 0.0))
    out_ref[...] = dot(k_high, d_high) + dot(k_high, d_low) + dot(k_low, d_high)


def forward_kernel(
    x_ref, c_ref, dy_ref, growth_ref, inner_ref, grad_c_ref, before_ref, decay_ref, start_ref,
    skip_ref, expand_ref, collect_ref, own_ref, other_ref, dots_ref,
):
    grow, c = dot(growth_ref[...], expand_ref[...]), c_ref[...]
    grown = dy_ref[...].astype(F32) * grow
    d_high, d_low = split2(grown)
    s_high, s_low = split2(before_ref[...] + decay_ref[...] * start_ref[...])
    inner = inner_ref[...] + dot(c, s_high) + dot(c, s_low)
    grad_c = grad_c_ref[...] + dot_nt(d_high, s_high) + dot_nt(d_high, s_low) + dot_nt(d_low, s_high)
    dots_ref[...] = gather_heads(grown * inner, collect_ref[...])
    y = inner * grow + skip_ref[...] * x_ref[...].astype(F32)
    y, grad_c = y.astype(BF16), grad_c.astype(BF16)
    result = jnp.concatenate([y, grad_c], axis=1)
    core_halves(result[: BLOCK // 2], result[BLOCK // 2 :], own_ref, other_ref)


def backward_kernel(
    x_ref, b_ref, dt_ref, dy_ref, weight_ref, inner_ref, grad_b_ref, later_ref, decay_ref, end_ref,
    final_ref, dots_ref, rate_ref, skip_ref, expand_ref, collect_ref,
    out_ref, rate_grad_ref, after,
):
    channels, width = x_ref.shape[1], b_ref.shape[1]

    @pl.when(pl.program_id(0) == 0)
    def _():
        meet = jnp.sum(final_ref[...] * end_ref[...], axis=0, keepdims=True)
        after[...] = gather_heads(jnp.broadcast_to(meet, (8, channels)), collect_ref[...])
        rate_grad_ref[...] = jnp.zeros_like(rate_grad_ref)

    b, weigh = b_ref[...], dot(weight_ref[...], expand_ref[...])
    scaled = x_ref[...].astype(F32) * weigh
    x_high, x_low = split2(scaled)
    g_high, g_low = split2(later_ref[...] + decay_ref[...] * end_ref[...])
    inner = inner_ref[...] + dot(b, g_high) + dot(b, g_low)
    pulled = gather_heads(scaled * inner, collect_ref[...])
    out_ref[:, :channels] = (inner * weigh + skip_ref[...] * dy_ref[...].astype(F32)).astype(BF16)
    grad_b = grad_b_ref[...] + dot_nt(x_high, g_high) + dot_nt(x_high, g_low) + dot_nt(x_low, g_high)
    out_ref[:, channels : channels + width] = grad_b.astype(BF16)
    dt = dt_ref[...].astype(F32)
    step, log_decay = step_sizes(dt, rate_ref[...])
    change = dots_ref[...] - pulled
    onward = (iota((BLOCK, BLOCK), 0) <= iota((BLOCK, BLOCK), 1)).astype(BF16)
    grad_log_decay = dot3(onward, change) + after[:1]
    after[...] = after[...] + jnp.sum(change, axis=0, keepdims=True)
    rate_grad_ref[...] += jnp.sum(grad_log_decay * log_decay, axis=0, keepdims=True)
    grad_step = pulled / step - rate_ref[...] * grad_log_decay
    out_ref[:, channels + width :] = (grad_step / (1.0 + jnp.exp(-dt))).astype(BF16)


def scan_kernel(heads, pieces_ref, expand_ref, out_ref, decay_ref):
    count, channels = out_ref.shape[0], out_ref.shape[2]
    decay_ref[...] = dot(three_terms(pieces_ref[:, 0, channels:], heads), expand_ref[...])
    total = jnp.zeros(out_ref.shape[1:], F32)
    for index in range(count):
        out_ref[index] = total
        total = total * decay_ref[index : index + 1] + pieces_ref[index, :, :channels]


def back_scan_kernel(pieces_ref, decay_ref, out_ref):
    total = jnp.zeros(out_ref.shape[1:], F32)
    for index in reversed(range(out_ref.shape[0])):
        out_ref[index] = total
        total = total * decay_ref[index : index + 1] + pieces_ref[index]


def params(mebibytes=VMEM_BYTES >> 20):
    return pltpu.CompilerParams(vmem_limit_bytes=mebibytes << 20, dimension_semantics=("arbitrary",))


def cost(flops, traffic):
    return pl.CostEstimate(flops=flops, bytes_accessed=traffic, transcendentals=0)


def seg_exchange(state):
    count = lax.axis_size("seg")
    return lax.all_to_all(state.reshape(count, -1, state.shape[-1]), "seg", 0, 0)


def seg_sum(value):
    count, hop = lax.axis_size("seg"), 1
    while hop < count:
        value = value + lax.ppermute(value, "seg", [(i, i ^ hop) for i in range(count)])
        hop *= 2
    return value


def exchange(value):
    return lax.all_to_all(value, "head", 0, 0)


def swap_cores(own, other):
    count = lax.axis_size("head")
    chips, rows, columns = own.shape
    swapped = lax.ppermute(other, "head", [(i, i ^ 1) for i in range(count)])
    return pl.pallas_call(
        merge_kernel,
        out_shape=[jax.ShapeDtypeStruct((2 * rows, columns), BF16)] * chips,
        compiler_params=pltpu.CompilerParams(vmem_limit_bytes=VMEM_BYTES),
        cost_estimate=cost(rows, 16 * own.size),
    )(own, swapped)


def swap_chips(sent, between):
    count = lax.axis_size("head")

    def permute(hop, value):
        return lax.ppermute(value, "head", [(i, (i + 2 * hop) % count) for i in range(count)])

    came = {0: sent[0], 1: permute(1, sent[1]), len(sent) - 1: permute(len(sent) - 1, sent[-1])}
    for hop in range(2, len(sent) - 1):
        value, *_ = lax.optimization_barrier((sent[hop], list(came.values())[1:], between))
        came[hop] = permute(hop, value)
    return [came[hop] for hop in range(len(sent))]


def on_device(inputs, b_rows, c_rows, dt_rows, a_log, d_skip, grad_out):
    shards, segments = lax.axis_size("head"), lax.axis_size("seg")
    rows = inputs.shape[0]
    heads = dt_rows.shape[1] // shards
    channels = inputs.shape[1] // shards
    width = b_rows.shape[1] // shards
    copies = LANES // heads
    first = lax.axis_index("head") * heads
    rate = jnp.exp(a_log)
    rate_here = lax.dynamic_slice_in_dim(rate, first, heads, 0)
    skip_here = lax.dynamic_slice_in_dim(d_skip, first, heads, 0)

    packed_width, pair_width = channels + width + LANES, channels + width
    packed = pl.pallas_call(
        lambda *refs: pack_kernel(heads, *refs),
        grid=(shards // 4,),
        in_specs=[
            pl.BlockSpec((rows, 4 * channels), lambda i: (0, i)),
            pl.BlockSpec((rows, 4 * width), lambda i: (0, i)),
            pl.BlockSpec((rows, LANES), lambda i: (0, 0)),
        ],
        out_specs=pl.BlockSpec((4, rows, packed_width), lambda i: (i, 0, 0)),
        out_shape=jax.ShapeDtypeStruct((shards, rows, packed_width), BF16),
        compiler_params=params(61),
        cost_estimate=cost(rows, 4 * shards * rows * packed_width),
    )(inputs, b_rows, dt_rows)
    first_in = exchange(packed)
    half_spec = pl.BlockSpec((None, rows, pair_width), lambda i: (i, 0, 0))
    half_shape = jax.ShapeDtypeStruct((shards // 2, rows, pair_width), BF16)
    own, other = pl.pallas_call(
        pack_pair_kernel,
        grid=(shards // 2,),
        in_specs=[
            pl.BlockSpec((rows, 2 * channels), lambda i: (0, i)),
            pl.BlockSpec((rows, 2 * width), lambda i: (0, i)),
        ],
        out_specs=[half_spec, half_spec],
        out_shape=[half_shape, half_shape],
        compiler_params=params(),
        cost_estimate=cost(rows, 4 * shards * rows * pair_width),
    )(grad_out, c_rows)
    first_in, sent = lax.optimization_barrier((first_in, swap_cores(own, other)))
    second_in = swap_chips(sent, None)

    length = rows * shards
    blocks = length // BLOCK
    xbd = first_in.reshape(length, packed_width)
    rate_row = jnp.tile(rate_here, copies)[None]
    skip_row = jnp.repeat(skip_here, HEAD_DIM)[None]
    lane, channel = jnp.arange(LANES), jnp.arange(channels)
    same = (lane % heads)[:, None] == (channel // HEAD_DIM)[None, :]
    expand = (same & (lane < 3 * heads)[:, None]).astype(BF16)
    collect = same.T.astype(BF16)

    def whole(array):
        return pl.BlockSpec(array.shape, lambda i: (0,) * array.ndim)

    def sections(place):
        return {
            "main": pl.BlockSpec((BLOCK, channels), lambda i: (place(i), 0)),
            "side": pl.BlockSpec((BLOCK, width), lambda i: (place(i), channels // width)),
            "dt": pl.BlockSpec((BLOCK, LANES), lambda i: (place(i), (channels + width) // LANES)),
            "per_head": pl.BlockSpec((BLOCK, LANES), lambda i: (place(i), 0)),
            "mixed": pl.BlockSpec((BLOCK, BLOCK), lambda i: (place(i), 0)),
            "decay": pl.BlockSpec((None, 1, channels), lambda i: (place(i), 0, 0)),
            "state": pl.BlockSpec((None, width, channels), lambda i: (place(i), 0, 0)),
        }

    onward = sections(lambda i: i)
    back = sections(lambda i: blocks - 1 - i)
    state_shape = jax.ShapeDtypeStruct((width, channels), F32)
    states_shape = jax.ShapeDtypeStruct((blocks, width, channels), F32)
    terms_shape = jax.ShapeDtypeStruct((length, LANES), BF16)
    main_shape = jax.ShapeDtypeStruct((length, channels), BF16)
    decays_shape = jax.ShapeDtypeStruct((blocks, 1, channels), F32)
    row_scratch = pltpu.VMEM((1, channels), F32)
    unit = 2 * length * width * channels

    state, growth, weight, x_high, x_low, before, decay_before = pl.pallas_call(
        lambda *refs: state_kernel(heads, *refs),
        grid=(blocks,),
        in_specs=[
            onward["main"], onward["side"],
            pl.BlockSpec((length, LANES), lambda i: (0, (channels + width) // LANES)),
            whole(rate_row), whole(expand),
        ],
        out_specs=[
            pl.BlockSpec((width, channels + LANES), lambda i: (0, 0)),
            pl.BlockSpec((length, LANES), lambda i: (0, 0)),
            pl.BlockSpec((length, LANES), lambda i: (0, 0)),
            onward["main"], onward["main"], onward["state"], onward["decay"],
        ],
        out_shape=[
            jax.ShapeDtypeStruct((width, channels + LANES), F32),
            terms_shape, terms_shape, main_shape, main_shape, states_shape, decays_shape,
        ],
        scratch_shapes=[row_scratch],
        compiler_params=params(),
        cost_estimate=cost(6 * unit, 4 * length * channels),
    )(xbd, xbd, xbd, rate_row, expand)
    piece = (segments, width // segments, channels)
    starts, decays = pl.pallas_call(
        lambda *refs: scan_kernel(heads, *refs),
        out_shape=[jax.ShapeDtypeStruct(piece, F32), jax.ShapeDtypeStruct((segments, channels), F32)],
        compiler_params=pltpu.CompilerParams(vmem_limit_bytes=VMEM_BYTES),
        cost_estimate=cost(unit, 8 * width * channels),
    )(seg_exchange(state), expand)
    starts, _ = lax.optimization_barrier((starts, second_in[1:]))
    start = seg_exchange(starts).reshape(width, channels)

    grad_state, dyc, d_high, d_low, later, decay_after = pl.pallas_call(
        lambda *refs: grad_state_kernel(len(second_in), *refs),
        grid=(blocks,),
        in_specs=[back["per_head"], whole(expand)] + [whole(part) for part in second_in],
        out_specs=[
            pl.BlockSpec((width, channels), lambda i: (0, 0)),
            pl.BlockSpec((BLOCK, pair_width), lambda i: (blocks - 1 - i, 0)),
            back["main"], back["main"], back["state"], back["decay"],
        ],
        out_shape=[
            state_shape, jax.ShapeDtypeStruct((length, pair_width), BF16),
            main_shape, main_shape, states_shape, decays_shape,
        ],
        scratch_shapes=[row_scratch],
        compiler_params=params(),
        cost_estimate=cost(6 * unit, 4 * length * channels),
    )(growth, expand, *second_in)
    inner, inside_b, inside_c, skip_grad = pl.pallas_call(
        inside_kernel,
        grid=(blocks,),
        in_specs=[onward[name] for name in ("main", "main", "main", "side", "main", "main", "main", "side")],
        out_specs=[
            onward["main"], onward["mixed"], onward["mixed"],
            pl.BlockSpec((1, channels), lambda i: (0, 0)),
        ],
        out_shape=[
            jax.ShapeDtypeStruct((length, channels), F32),
            jax.ShapeDtypeStruct((length, width), F32), jax.ShapeDtypeStruct((length, width), F32),
            jax.ShapeDtypeStruct((1, channels), F32),
        ],
        compiler_params=params(61),
        cost_estimate=cost(8 * unit, 16 * length * channels),
    )(xbd, x_high, x_low, xbd, dyc, d_high, d_low, dyc)

    grad_state, _ = lax.optimization_barrier((grad_state, (start, inner)))
    pieces = seg_exchange(grad_state)
    own, other, dots = pl.pallas_call(
        forward_kernel,
        grid=(blocks,),
        in_specs=[
            onward["main"], onward["side"], onward["main"], onward["per_head"],
            onward["main"], onward["mixed"], onward["state"], onward["decay"],
            whole(start), whole(skip_row), whole(expand), whole(collect),
        ],
        out_specs=[half_spec, half_spec, onward["per_head"]],
        out_shape=[half_shape, half_shape, jax.ShapeDtypeStruct((length, LANES), F32)],
        compiler_params=params(),
        cost_estimate=cost(8 * unit, 16 * length * channels),
    )(xbd, dyc, dyc, growth, inner, inside_c, before, decay_before, start, skip_row, expand, collect)
    ends = pl.pallas_call(
        back_scan_kernel,
        out_shape=jax.ShapeDtypeStruct(piece, F32),
        compiler_params=pltpu.CompilerParams(vmem_limit_bytes=VMEM_BYTES),
        cost_estimate=cost(unit, 8 * width * channels),
    )(pieces, decays)
    own, other, _ = lax.optimization_barrier((own, other, pieces))
    d_high, _ = lax.optimization_barrier((d_high, pieces))
    total = lax.dynamic_slice_in_dim(decays, lax.axis_index("seg"), 1, 0)
    slab = pl.BlockSpec((width // blocks, channels), lambda i: (i, 0))
    grad_inner, final = pl.pallas_call(
        inside_grad_kernel,
        grid=(blocks,),
        in_specs=[onward[name] for name in ("side", "main", "main", "side")] + [slab, slab, whole(total)],
        out_specs=[onward["main"], slab],
        out_shape=[jax.ShapeDtypeStruct((length, channels), F32), state_shape],
        compiler_params=params(),
        cost_estimate=cost(4 * unit, 8 * length * channels),
    )(xbd, d_high, d_low, dyc, state, start, total)
    first_out = swap_chips(swap_cores(own, other), grad_inner)
    end = seg_exchange(ends).reshape(width, channels)


    grads, rate_grad = pl.pallas_call(
        backward_kernel,
        grid=(blocks,),
        in_specs=[
            back["main"], back["side"], back["dt"], back["main"], back["per_head"],
            back["main"], back["mixed"], back["state"], back["decay"],
            whole(end), whole(final),
            back["per_head"], whole(rate_row), whole(skip_row), whole(expand), whole(collect),
        ],
        out_specs=[
            pl.BlockSpec((BLOCK, packed_width), lambda i: (blocks - 1 - i, 0)),
            pl.BlockSpec((1, LANES), lambda i: (0, 0)),
        ],
        out_shape=[
            jax.ShapeDtypeStruct((length, packed_width), BF16),
            jax.ShapeDtypeStruct((1, LANES), F32),
        ],
        scratch_shapes=[pltpu.VMEM((8, LANES), F32)],
        compiler_params=params(61),
        cost_estimate=cost(8 * unit, 16 * length * channels),
    )(
        xbd, xbd, xbd, dyc, weight, grad_inner, inside_b, later, decay_after,
        end, final, dots, rate_row, skip_row, expand, collect,
    )
    grads, _ = lax.optimization_barrier((grads, first_out[1:]))
    second_out = exchange(grads.reshape(shards, rows, packed_width))

    skip_grad = skip_grad.reshape(heads, HEAD_DIM).sum(axis=1)
    sums = jnp.concatenate([rate_grad[0, :heads], skip_grad])
    sums = seg_sum(jnp.pad(sums, (0, LANES - 2 * heads))[None])[0]

    grad_x, grad_b, grad_dt = pl.pallas_call(
        lambda *refs: unpack_kernel(heads, *refs),
        grid=(shards // 2,),
        in_specs=[pl.BlockSpec((2, rows, packed_width), lambda i: (i, 0, 0))],
        out_specs=[
            pl.BlockSpec((rows, 2 * channels), lambda i: (0, i)),
            pl.BlockSpec((rows, 2 * width), lambda i: (0, i)),
            pl.BlockSpec((rows, LANES), lambda i: (0, 0)),
        ],
        out_shape=[jax.ShapeDtypeStruct(like.shape, BF16) for like in (inputs, b_rows, dt_rows)],
        compiler_params=params(),
        cost_estimate=cost(rows, 4 * shards * rows * packed_width),
    )(second_out)
    outputs, grad_c = pl.pallas_call(
        lambda *refs: unpack_pairs_kernel(len(first_out), *refs),
        out_shape=[jax.ShapeDtypeStruct(like.shape, BF16) for like in (inputs, c_rows)],
        compiler_params=pltpu.CompilerParams(vmem_limit_bytes=VMEM_BYTES),
        cost_estimate=cost(rows, 4 * shards * rows * pair_width),
    )(*first_out)
    return outputs, grad_x, grad_b, grad_c, grad_dt, sums[:heads], sums[heads : 2 * heads]


def solution(mesh):
    by_rows = P(("dp", "seg", "head"), None)
    in_specs = (by_rows, by_rows, by_rows, by_rows, P(), P(), by_rows)
    out_specs = (by_rows, by_rows, by_rows, by_rows, by_rows, P(("dp", "head")), P(("dp", "head")))
    return jax.shard_map(on_device, mesh=mesh, in_specs=in_specs, out_specs=out_specs, check_vma=False)
```

```python
import jax
import jax.numpy as jnp
from jax import lax
from jax.experimental import pallas as pl
from jax.experimental.pallas import tpu as pltpu
from jax.sharding import PartitionSpec as P

HEAD_DIM = 64
GSTATE = 256
BLOCK = 256
LANES = 128
CHANNELS = 1024
VMEM_BYTES = 50 * 1024 * 1024

F32 = jnp.float32
BF16 = jnp.bfloat16


def dot(left, right):
    return lax.dot_general(left, right, (((1,), (0,)), ((), ())), preferred_element_type=F32)


def dot_nt(left, right):
    return lax.dot_general(left, right, (((1,), (1,)), ((), ())), preferred_element_type=F32)


def split2(value):
    high = value.astype(BF16)
    return high, (value - high.astype(F32)).astype(BF16)


def split3(value):
    high, rest = value.astype(BF16), None
    rest = value - high.astype(F32)
    middle = rest.astype(BF16)
    return high, middle, (rest - middle.astype(F32)).astype(BF16)


def dot3(ones, value):
    high, middle, low = split3(value)
    return dot(ones, high) + dot(ones, middle) + dot(ones, low)


def iota(shape, dim):
    return lax.broadcasted_iota(jnp.int32, shape, dim)


def step_sizes(dt, rate):
    step = jnp.log(1.0 + jnp.exp(dt))
    return step, -step * rate


def three_terms(value, heads):
    high, middle, low = split3(value)
    lane = iota(value.shape, 1)
    return jnp.where(lane < heads, high, jnp.where(lane < 2 * heads, middle, low))


def gather_heads(value, collect):
    high, low = split2(value)
    return dot(high, collect) + dot(low, collect)


def pack_kernel(heads, x_ref, b_ref, dt_ref, out_ref):
    here, channels, width = out_ref.shape[0], CHANNELS, GSTATE
    for index in range(here):
        shard = pl.program_id(0) * here + index
        out_ref[index, :, :channels] = x_ref[:, index * channels : (index + 1) * channels]
        out_ref[index, :, channels : channels + width] = b_ref[:, index * width : (index + 1) * width]
        wanted = shard * heads + lax.rem(iota((LANES, LANES), 1), heads)
        pick = (iota((LANES, LANES), 0) == wanted).astype(BF16)
        out_ref[index, :, channels + width :] = dot(dt_ref[...], pick).astype(BF16)


def unpack_kernel(heads, in_ref, x_ref, b_ref, dt_ref):
    here, channels, width = in_ref.shape[0], CHANNELS, GSTATE
    for index in range(here):
        shard = pl.program_id(0) * here + index
        x_ref[:, index * channels : (index + 1) * channels] = in_ref[index, :, :channels]
        b_ref[:, index * width : (index + 1) * width] = in_ref[index, :, channels : channels + width]
        mine = iota(dt_ref.shape, 1) // heads == shard
        dt_ref[...] = jnp.where(mine, in_ref[index, :, channels + width :], dt_ref[...])


def core_halves(first, second, own_ref, other_ref):
    core = lax.rem(lax.axis_index("head"), 2)

    @pl.when(core == 0)
    def _():
        own_ref[...], other_ref[...] = first, second

    @pl.when(core == 1)
    def _():
        own_ref[...], other_ref[...] = second, first


def pack_pair_kernel(dy_ref, c_ref, own_ref, other_ref):
    channels, width = CHANNELS, GSTATE
    first = jnp.concatenate([dy_ref[:, :channels], c_ref[:, :width]], axis=1)
    second = jnp.concatenate([dy_ref[:, channels:], c_ref[:, width:]], axis=1)
    core_halves(first, second, own_ref, other_ref)


def merge_kernel(own_ref, swapped_ref, *out_refs):
    me, chips, rows = lax.axis_index("head"), own_ref.shape[0], own_ref.shape[1]
    core = lax.rem(me, 2)
    for hop, out_ref in enumerate(out_refs):
        chip = lax.rem(me // 2 + hop, chips)
        out_ref[pl.ds(pl.multiple_of(core * rows, rows), rows), :] = own_ref[chip]
        out_ref[pl.ds(pl.multiple_of((1 - core) * rows, rows), rows), :] = swapped_ref[chip]


def unpack_pairs_kernel(pieces, *refs):
    piece_refs, (y_ref, c_ref) = refs[:pieces], refs[pieces:]
    me, rows, channels, width = lax.axis_index("head"), y_ref.shape[0], CHANNELS, GSTATE
    for hop, piece_ref in enumerate(piece_refs):
        chip = lax.rem(me // 2 - hop + pieces, pieces)
        for core in range(2):
            part = slice(core * rows, (core + 1) * rows)
            at = pl.multiple_of((2 * chip + core) * channels, channels)
            y_ref[:, pl.ds(at, channels)] = piece_ref[part, :channels]
            at = pl.multiple_of((2 * chip + core) * width, width)
            c_ref[:, pl.ds(at, width)] = piece_ref[part, channels:]


def state_kernel(
    heads, x_ref, b_ref, dt_ref, rate_ref, expand_ref,
    out_ref, growth_ref, weight_ref, high_ref, low_ref, before_ref, decay_ref, so_far,
):
    block = pl.program_id(0)
    channels = x_ref.shape[1]

    @pl.when(block == 0)
    def _():
        out_ref[...] = jnp.zeros_like(out_ref)
        so_far[...] = jnp.ones_like(so_far)
        lower = (iota((BLOCK, BLOCK), 0) >= iota((BLOCK, BLOCK), 1)).astype(BF16)
        log_total = jnp.zeros((1, LANES), F32)
        for at in range(0, dt_ref.shape[0], BLOCK):
            rows = slice(at, at + BLOCK)
            step, log_decay = step_sizes(dt_ref[rows].astype(F32), rate_ref[...])
            cumulative = dot3(lower, log_decay)
            growth_ref[rows] = three_terms(jnp.exp(cumulative), heads)
            weight_ref[rows] = three_terms(jnp.exp(-cumulative) * step, heads)
            log_total = log_total + cumulative[BLOCK - 1 :]
        out_ref[:, channels:] = jnp.broadcast_to(jnp.exp(log_total), (out_ref.shape[0], LANES))

    rows = pl.ds(pl.multiple_of(block * BLOCK, BLOCK), BLOCK)
    ends = pl.ds(pl.multiple_of(block * BLOCK + BLOCK - 16, 16), 16)
    spread = expand_ref[...]
    high, low = split2(x_ref[...].astype(F32) * dot(weight_ref[rows, :], spread))
    high_ref[...], low_ref[...] = high, low
    decay = dot(growth_ref[ends, :], spread)[15:]
    b_t = b_ref[...].T
    state = out_ref[:, :channels]
    before_ref[...] = state
    decay_ref[...] = so_far[...]
    so_far[...] = so_far[...] * decay
    out_ref[:, :channels] = (state + dot(b_t, high) + dot(b_t, low)) * decay


def grad_state_kernel(pieces, growth_ref, expand_ref, *refs):
    piece_refs, (out_ref, dyc_ref, high_ref, low_ref, later_ref, decay_ref, so_far) = refs[:pieces], refs[pieces:]
    channels = out_ref.shape[1]
    block = pl.num_programs(0) - 1 - pl.program_id(0)
    hop = lax.rem(lax.axis_index("head") // 2 - block + pieces, pieces)

    @pl.when(pl.program_id(0) == 0)
    def _():
        out_ref[...] = jnp.zeros_like(out_ref)
        so_far[...] = jnp.ones_like(so_far)

    for index, piece_ref in enumerate(piece_refs):
        @pl.when(hop == index)
        def _():
            dyc_ref[...] = piece_ref[...]

    grow = dot(growth_ref[...], expand_ref[...])
    decay = grow[BLOCK - 1 :]
    high, low = split2(dyc_ref[:, :channels].astype(F32) * grow)
    high_ref[...], low_ref[...] = high, low
    c_t = dyc_ref[:, channels:].T
    later = out_ref[...] * decay
    later_ref[...] = later
    so_far[...] = so_far[...] * decay
    decay_ref[...] = so_far[...]
    out_ref[...] = later + dot(c_t, high) + dot(c_t, low)


def inside_kernel(
    x_ref, x_high_ref, x_low_ref, b_ref, dy_ref, d_high_ref, d_low_ref, c_ref,
    inner_ref, grad_b_ref, grad_c_ref, skip_grad_ref,
):
    @pl.when(pl.program_id(0) == 0)
    def _():
        skip_grad_ref[...] = jnp.zeros_like(skip_grad_ref)

    b, c = b_ref[...], c_ref[...]
    skip_grad_ref[...] += jnp.sum(dy_ref[...].astype(F32) * x_ref[...].astype(F32), axis=0, keepdims=True)
    x_high, x_low, d_high, d_low = x_high_ref[...], x_low_ref[...], d_high_ref[...], d_low_ref[...]
    causal = iota((BLOCK, BLOCK), 0) >= iota((BLOCK, BLOCK), 1)
    k_high, k_low = split2(jnp.where(causal, dot_nt(c, b), 0.0))
    inner_ref[...] = dot(k_high, x_high) + dot(k_high, x_low) + dot(k_low, x_high)
    mixed = dot_nt(d_high, x_high) + dot_nt(d_high, x_low) + dot_nt(d_low, x_high)
    mixed = jnp.where(causal, mixed, 0.0)
    q_high, q_low = split2(mixed)
    grad_c_ref[...] = dot(q_high, b) + dot(q_low, b)
    q_high, q_low = split2(mixed.T)
    grad_b_ref[...] = dot(q_high, c) + dot(q_low, c)


def inside_grad_kernel(b_ref, d_high_ref, d_low_ref, c_ref, state_ref, start_ref, total_ref, out_ref, final_ref):
    final_ref[...] = state_ref[...] + total_ref[...] * start_ref[...]
    d_high, d_low = d_high_ref[...], d_low_ref[...]
    anticausal = iota((BLOCK, BLOCK), 0) <= iota((BLOCK, BLOCK), 1)
    k_high, k_low = split2(jnp.where(anticausal, dot_nt(b_ref[...], c_ref[...]), 0.0))
    out_ref[...] = dot(k_high, d_high) + dot(k_high, d_low) + dot(k_low, d_high)


def forward_kernel(
    x_ref, c_ref, dy_ref, growth_ref, inner_ref, grad_c_ref, before_ref, decay_ref, start_ref,
    skip_ref, expand_ref, collect_ref, own_ref, other_ref, dots_ref,
):
    grow, c = dot(growth_ref[...], expand_ref[...]), c_ref[...]
    grown = dy_ref[...].astype(F32) * grow
    d_high, d_low = split2(grown)
    s_high, s_low = split2(before_ref[...] + decay_ref[...] * start_ref[...])
    inner = inner_ref[...] + dot(c, s_high) + dot(c, s_low)
    grad_c = grad_c_ref[...] + dot_nt(d_high, s_high) + dot_nt(d_high, s_low) + dot_nt(d_low, s_high)
    dots_ref[...] = gather_heads(grown * inner, collect_ref[...])
    y = inner * grow + skip_ref[...] * x_ref[...].astype(F32)
    y, grad_c = y.astype(BF16), grad_c.astype(BF16)
    result = jnp.concatenate([y, grad_c], axis=1)
    core_halves(result[: BLOCK // 2], result[BLOCK // 2 :], own_ref, other_ref)


def backward_kernel(
    x_ref, b_ref, dt_ref, dy_ref, weight_ref, inner_ref, grad_b_ref, later_ref, decay_ref, end_ref,
    final_ref, dots_ref, rate_ref, skip_ref, expand_ref, collect_ref,
    out_ref, rate_grad_ref, after,
):
    channels, width = x_ref.shape[1], b_ref.shape[1]

    @pl.when(pl.program_id(0) == 0)
    def _():
        meet = jnp.sum(final_ref[...] * end_ref[...], axis=0, keepdims=True)
        after[...] = gather_heads(jnp.broadcast_to(meet, (8, channels)), collect_ref[...])
        rate_grad_ref[...] = jnp.zeros_like(rate_grad_ref)

    b, weigh = b_ref[...], dot(weight_ref[...], expand_ref[...])
    scaled = x_ref[...].astype(F32) * weigh
    x_high, x_low = split2(scaled)
    g_high, g_low = split2(later_ref[...] + decay_ref[...] * end_ref[...])
    inner = inner_ref[...] + dot(b, g_high) + dot(b, g_low)
    pulled = gather_heads(scaled * inner, collect_ref[...])
    out_ref[:, :channels] = (inner * weigh + skip_ref[...] * dy_ref[...].astype(F32)).astype(BF16)
    grad_b = grad_b_ref[...] + dot_nt(x_high, g_high) + dot_nt(x_high, g_low) + dot_nt(x_low, g_high)
    out_ref[:, channels : channels + width] = grad_b.astype(BF16)
    dt = dt_ref[...].astype(F32)
    step, log_decay = step_sizes(dt, rate_ref[...])
    change = dots_ref[...] - pulled
    onward = (iota((BLOCK, BLOCK), 0) <= iota((BLOCK, BLOCK), 1)).astype(BF16)
    grad_log_decay = dot3(onward, change) + after[:1]
    after[...] = after[...] + jnp.sum(change, axis=0, keepdims=True)
    rate_grad_ref[...] += jnp.sum(grad_log_decay * log_decay, axis=0, keepdims=True)
    grad_step = pulled / step - rate_ref[...] * grad_log_decay
    out_ref[:, channels + width :] = (grad_step / (1.0 + jnp.exp(-dt))).astype(BF16)


def scan_kernel(heads, pieces_ref, expand_ref, out_ref, decay_ref):
    count, channels = out_ref.shape[0], out_ref.shape[2]
    decay_ref[...] = dot(three_terms(pieces_ref[:, 0, channels:], heads), expand_ref[...])
    total = jnp.zeros(out_ref.shape[1:], F32)
    for index in range(count):
        out_ref[index] = total
        total = total * decay_ref[index : index + 1] + pieces_ref[index, :, :channels]


def back_scan_kernel(pieces_ref, decay_ref, out_ref):
    total = jnp.zeros(out_ref.shape[1:], F32)
    for index in reversed(range(out_ref.shape[0])):
        out_ref[index] = total
        total = total * decay_ref[index : index + 1] + pieces_ref[index]


def params(mebibytes=VMEM_BYTES >> 20):
    return pltpu.CompilerParams(vmem_limit_bytes=mebibytes << 20, dimension_semantics=("arbitrary",))


def cost(flops, traffic):
    return pl.CostEstimate(flops=flops, bytes_accessed=traffic, transcendentals=0)


def seg_exchange(state):
    count = lax.axis_size("seg")
    return lax.all_to_all(state.reshape(count, -1, state.shape[-1]), "seg", 0, 0)


def seg_sum(value):
    count, hop = lax.axis_size("seg"), 1
    while hop < count:
        value = value + lax.ppermute(value, "seg", [(i, i ^ hop) for i in range(count)])
        hop *= 2
    return value


def exchange(value):
    return lax.all_to_all(value, "head", 0, 0)


def swap_cores(own, other):
    count = lax.axis_size("head")
    chips, rows, columns = own.shape
    swapped = lax.ppermute(other, "head", [(i, i ^ 1) for i in range(count)])
    return pl.pallas_call(
        merge_kernel,
        out_shape=[jax.ShapeDtypeStruct((2 * rows, columns), BF16)] * chips,
        compiler_params=pltpu.CompilerParams(vmem_limit_bytes=VMEM_BYTES),
        cost_estimate=cost(rows, 16 * own.size),
    )(own, swapped)


def swap_chips(sent, between):
    count = lax.axis_size("head")

    def permute(hop, value):
        return lax.ppermute(value, "head", [(i, (i + 2 * hop) % count) for i in range(count)])

    came = {0: sent[0], 1: permute(1, sent[1]), len(sent) - 1: permute(len(sent) - 1, sent[-1])}
    for hop in range(2, len(sent) - 1):
        value, *_ = lax.optimization_barrier((sent[hop], list(came.values())[1:], between))
        came[hop] = permute(hop, value)
    return [came[hop] for hop in range(len(sent))]


def on_device(inputs, b_rows, c_rows, dt_rows, a_log, d_skip, grad_out):
    shards, segments = lax.axis_size("head"), lax.axis_size("seg")
    rows = inputs.shape[0]
    heads = dt_rows.shape[1] // shards
    channels = inputs.shape[1] // shards
    width = b_rows.shape[1] // shards
    copies = LANES // heads
    first = lax.axis_index("head") * heads
    rate = jnp.exp(a_log)
    rate_here = lax.dynamic_slice_in_dim(rate, first, heads, 0)
    skip_here = lax.dynamic_slice_in_dim(d_skip, first, heads, 0)

    packed_width, pair_width = channels + width + LANES, channels + width
    packed = pl.pallas_call(
        lambda *refs: pack_kernel(heads, *refs),
        grid=(shards // 4,),
        in_specs=[
            pl.BlockSpec((rows, 4 * channels), lambda i: (0, i)),
            pl.BlockSpec((rows, 4 * width), lambda i: (0, i)),
            pl.BlockSpec((rows, LANES), lambda i: (0, 0)),
        ],
        out_specs=pl.BlockSpec((4, rows, packed_width), lambda i: (i, 0, 0)),
        out_shape=jax.ShapeDtypeStruct((shards, rows, packed_width), BF16),
        compiler_params=params(61),
        cost_estimate=cost(rows, 4 * shards * rows * packed_width),
    )(inputs, b_rows, dt_rows)
    first_in = exchange(packed)
    half_spec = pl.BlockSpec((None, rows, pair_width), lambda i: (i, 0, 0))
    half_shape = jax.ShapeDtypeStruct((shards // 2, rows, pair_width), BF16)
    own, other = pl.pallas_call(
        pack_pair_kernel,
        grid=(shards // 2,),
        in_specs=[
            pl.BlockSpec((rows, 2 * channels), lambda i: (0, i)),
            pl.BlockSpec((rows, 2 * width), lambda i: (0, i)),
        ],
        out_specs=[half_spec, half_spec],
        out_shape=[half_shape, half_shape],
        compiler_params=params(),
        cost_estimate=cost(rows, 4 * shards * rows * pair_width),
    )(grad_out, c_rows)
    first_in, sent = lax.optimization_barrier((first_in, swap_cores(own, other)))
    second_in = swap_chips(sent, None)

    length = rows * shards
    blocks = length // BLOCK
    xbd = first_in.reshape(length, packed_width)
    rate_row = jnp.tile(rate_here, copies)[None]
    skip_row = jnp.repeat(skip_here, HEAD_DIM)[None]
    lane, channel = jnp.arange(LANES), jnp.arange(channels)
    same = (lane % heads)[:, None] == (channel // HEAD_DIM)[None, :]
    expand = (same & (lane < 3 * heads)[:, None]).astype(BF16)
    collect = same.T.astype(BF16)

    def whole(array):
        return pl.BlockSpec(array.shape, lambda i: (0,) * array.ndim)

    def sections(place):
        return {
            "main": pl.BlockSpec((BLOCK, channels), lambda i: (place(i), 0)),
            "side": pl.BlockSpec((BLOCK, width), lambda i: (place(i), channels // width)),
            "dt": pl.BlockSpec((BLOCK, LANES), lambda i: (place(i), (channels + width) // LANES)),
            "per_head": pl.BlockSpec((BLOCK, LANES), lambda i: (place(i), 0)),
            "mixed": pl.BlockSpec((BLOCK, BLOCK), lambda i: (place(i), 0)),
            "decay": pl.BlockSpec((None, 1, channels), lambda i: (place(i), 0, 0)),
            "state": pl.BlockSpec((None, width, channels), lambda i: (place(i), 0, 0)),
        }

    onward = sections(lambda i: i)
    back = sections(lambda i: blocks - 1 - i)
    state_shape = jax.ShapeDtypeStruct((width, channels), F32)
    states_shape = jax.ShapeDtypeStruct((blocks, width, channels), F32)
    terms_shape = jax.ShapeDtypeStruct((length, LANES), BF16)
    main_shape = jax.ShapeDtypeStruct((length, channels), BF16)
    decays_shape = jax.ShapeDtypeStruct((blocks, 1, channels), F32)
    row_scratch = pltpu.VMEM((1, channels), F32)
    unit = 2 * length * width * channels

    state, growth, weight, x_high, x_low, before, decay_before = pl.pallas_call(
        lambda *refs: state_kernel(heads, *refs),
        grid=(blocks,),
        in_specs=[
            onward["main"], onward["side"],
            pl.BlockSpec((length, LANES), lambda i: (0, (channels + width) // LANES)),
            whole(rate_row), whole(expand),
        ],
        out_specs=[
            pl.BlockSpec((width, channels + LANES), lambda i: (0, 0)),
            pl.BlockSpec((length, LANES), lambda i: (0, 0)),
            pl.BlockSpec((length, LANES), lambda i: (0, 0)),
            onward["main"], onward["main"], onward["state"], onward["decay"],
        ],
        out_shape=[
            jax.ShapeDtypeStruct((width, channels + LANES), F32),
            terms_shape, terms_shape, main_shape, main_shape, states_shape, decays_shape,
        ],
        scratch_shapes=[row_scratch],
        compiler_params=params(61),
        cost_estimate=cost(6 * unit, 4 * length * channels),
    )(xbd, xbd, xbd, rate_row, expand)
    piece = (segments, width // segments, channels)
    starts, decays = pl.pallas_call(
        lambda *refs: scan_kernel(heads, *refs),
        out_shape=[jax.ShapeDtypeStruct(piece, F32), jax.ShapeDtypeStruct((segments, channels), F32)],
        compiler_params=pltpu.CompilerParams(vmem_limit_bytes=VMEM_BYTES),
        cost_estimate=cost(unit, 8 * width * channels),
    )(seg_exchange(state), expand)
    starts, _ = lax.optimization_barrier((starts, second_in[1:]))
    start = seg_exchange(starts).reshape(width, channels)

    grad_state, dyc, d_high, d_low, later, decay_after = pl.pallas_call(
        lambda *refs: grad_state_kernel(len(second_in), *refs),
        grid=(blocks,),
        in_specs=[back["per_head"], whole(expand)] + [whole(part) for part in second_in],
        out_specs=[
            pl.BlockSpec((width, channels), lambda i: (0, 0)),
            pl.BlockSpec((BLOCK, pair_width), lambda i: (blocks - 1 - i, 0)),
            back["main"], back["main"], back["state"], back["decay"],
        ],
        out_shape=[
            state_shape, jax.ShapeDtypeStruct((length, pair_width), BF16),
            main_shape, main_shape, states_shape, decays_shape,
        ],
        scratch_shapes=[row_scratch],
        compiler_params=params(),
        cost_estimate=cost(6 * unit, 4 * length * channels),
    )(growth, expand, *second_in)
    inner, inside_b, inside_c, skip_grad = pl.pallas_call(
        inside_kernel,
        grid=(blocks,),
        in_specs=[onward[name] for name in ("main", "main", "main", "side", "main", "main", "main", "side")],
        out_specs=[
            onward["main"], onward["mixed"], onward["mixed"],
            pl.BlockSpec((1, channels), lambda i: (0, 0)),
        ],
        out_shape=[
            jax.ShapeDtypeStruct((length, channels), F32),
            jax.ShapeDtypeStruct((length, width), F32), jax.ShapeDtypeStruct((length, width), F32),
            jax.ShapeDtypeStruct((1, channels), F32),
        ],
        compiler_params=params(61),
        cost_estimate=cost(8 * unit, 16 * length * channels),
    )(xbd, x_high, x_low, xbd, dyc, d_high, d_low, dyc)

    grad_state, _ = lax.optimization_barrier((grad_state, (start, inner)))
    pieces = seg_exchange(grad_state)
    own, other, dots = pl.pallas_call(
        forward_kernel,
        grid=(blocks,),
        in_specs=[
            onward["main"], onward["side"], onward["main"], onward["per_head"],
            onward["main"], onward["mixed"], onward["state"], onward["decay"],
            whole(start), whole(skip_row), whole(expand), whole(collect),
        ],
        out_specs=[half_spec, half_spec, onward["per_head"]],
        out_shape=[half_shape, half_shape, jax.ShapeDtypeStruct((length, LANES), F32)],
        compiler_params=params(),
        cost_estimate=cost(8 * unit, 16 * length * channels),
    )(xbd, dyc, dyc, growth, inner, inside_c, before, decay_before, start, skip_row, expand, collect)
    ends = pl.pallas_call(
        back_scan_kernel,
        out_shape=jax.ShapeDtypeStruct(piece, F32),
        compiler_params=pltpu.CompilerParams(vmem_limit_bytes=VMEM_BYTES),
        cost_estimate=cost(unit, 8 * width * channels),
    )(pieces, decays)
    own, other, _ = lax.optimization_barrier((own, other, pieces))
    d_high, _ = lax.optimization_barrier((d_high, pieces))
    total = lax.dynamic_slice_in_dim(decays, lax.axis_index("seg"), 1, 0)
    slab = pl.BlockSpec((width // blocks, channels), lambda i: (i, 0))
    grad_inner, final = pl.pallas_call(
        inside_grad_kernel,
        grid=(blocks,),
        in_specs=[onward[name] for name in ("side", "main", "main", "side")] + [slab, slab, whole(total)],
        out_specs=[onward["main"], slab],
        out_shape=[jax.ShapeDtypeStruct((length, channels), F32), state_shape],
        compiler_params=params(),
        cost_estimate=cost(4 * unit, 8 * length * channels),
    )(xbd, d_high, d_low, dyc, state, start, total)
    first_out = swap_chips(swap_cores(own, other), grad_inner)
    end = seg_exchange(ends).reshape(width, channels)


    grads, rate_grad = pl.pallas_call(
        backward_kernel,
        grid=(blocks,),
        in_specs=[
            back["main"], back["side"], back["dt"], back["main"], back["per_head"],
            back["main"], back["mixed"], back["state"], back["decay"],
            whole(end), whole(final),
            back["per_head"], whole(rate_row), whole(skip_row), whole(expand), whole(collect),
        ],
        out_specs=[
            pl.BlockSpec((BLOCK, packed_width), lambda i: (blocks - 1 - i, 0)),
            pl.BlockSpec((1, LANES), lambda i: (0, 0)),
        ],
        out_shape=[
            jax.ShapeDtypeStruct((length, packed_width), BF16),
            jax.ShapeDtypeStruct((1, LANES), F32),
        ],
        scratch_shapes=[pltpu.VMEM((8, LANES), F32)],
        compiler_params=params(61),
        cost_estimate=cost(8 * unit, 16 * length * channels),
    )(
        xbd, xbd, xbd, dyc, weight, grad_inner, inside_b, later, decay_after,
        end, final, dots, rate_row, skip_row, expand, collect,
    )
    grads, _ = lax.optimization_barrier((grads, first_out[1:]))
    second_out = exchange(grads.reshape(shards, rows, packed_width))

    skip_grad = skip_grad.reshape(heads, HEAD_DIM).sum(axis=1)
    sums = jnp.concatenate([rate_grad[0, :heads], skip_grad])
    sums = seg_sum(jnp.pad(sums, (0, LANES - 2 * heads))[None])[0]

    grad_x, grad_b, grad_dt = pl.pallas_call(
        lambda *refs: unpack_kernel(heads, *refs),
        grid=(shards // 2,),
        in_specs=[pl.BlockSpec((2, rows, packed_width), lambda i: (i, 0, 0))],
        out_specs=[
            pl.BlockSpec((rows, 2 * channels), lambda i: (0, i)),
            pl.BlockSpec((rows, 2 * width), lambda i: (0, i)),
            pl.BlockSpec((rows, LANES), lambda i: (0, 0)),
        ],
        out_shape=[jax.ShapeDtypeStruct(like.shape, BF16) for like in (inputs, b_rows, dt_rows)],
        compiler_params=params(),
        cost_estimate=cost(rows, 4 * shards * rows * packed_width),
    )(second_out)
    outputs, grad_c = pl.pallas_call(
        lambda *refs: unpack_pairs_kernel(len(first_out), *refs),
        out_shape=[jax.ShapeDtypeStruct(like.shape, BF16) for like in (inputs, c_rows)],
        compiler_params=pltpu.CompilerParams(vmem_limit_bytes=VMEM_BYTES),
        cost_estimate=cost(rows, 4 * shards * rows * pair_width),
    )(*first_out)
    return outputs, grad_x, grad_b, grad_c, grad_dt, sums[:heads], sums[heads : 2 * heads]


def solution(mesh):
    by_rows = P(("dp", "seg", "head"), None)
    in_specs = (by_rows, by_rows, by_rows, by_rows, P(), P(), by_rows)
    out_specs = (by_rows, by_rows, by_rows, by_rows, by_rows, P(("dp", "head")), P(("dp", "head")))
    return jax.shard_map(on_device, mesh=mesh, in_specs=in_specs, out_specs=out_specs, check_vma=False)
```
